32 devices in a mesh: row: 4 (over y, x), col: 8 (over z, core).
Axes of the slice: x: 2, y: 2, z: 4, core: 2. Of those that a mesh axis runs over, the one named last changes fastest.
Arguments:
- matrix: float32 [4096, 4096], P('row', 'col'), may hold values from 0 to 9.5, as said below
Outputs:
- factored: float32 [4096, 4096], P('row', 'col')
The draws below stay inside these ranges and needn't reach their ends.
Inputs may be any that keep to these rules, and one draw needn't show every extreme that they name: `matrix`: symmetric positive definite once the block order is reverted.
All inputs are finite; a program needn't handle non-finite values.
Results may differ from the reference program's by a relative error of at most 0.0003.
Values sent between devices are 32-bit elements; how exact they have to be, the bound alone decides.
No kernel may reach another device: no remote copies, remote signals or barrier semaphores. Data moves between devices by JAX's collectives and lax.ppermute only.
A program may use at most 128 MiB of HBM per device.

```python
import jax
import jax.numpy as jnp
from jax import lax

NB = 256
BR = 4
PANELS = 3
BLOCKS = 16
BC = 2
ORDER = 4096


NUGGET = 0.5


SHOWN_RANGE = 0.2


def draw_matrix(key, part):
    place_key = jax.random.fold_in(jax.random.fold_in(key, 7), 0)
    locations = jax.random.uniform(place_key, (ORDER, 2), jnp.float32)
    length_scale = SHOWN_RANGE
    delta_x = locations[:, None, 0] - locations[None, :, 0]
    delta_y = locations[:, None, 1] - locations[None, :, 1]
    distance = jnp.sqrt(delta_x * delta_x + delta_y * delta_y)
    diagonal_ones = (lax.broadcasted_iota(jnp.int32, (ORDER, ORDER), 0) == lax.broadcasted_iota(jnp.int32, (ORDER, ORDER), 1)).astype(jnp.float32)
    covariance = jnp.exp(-distance / length_scale) + NUGGET * diagonal_ones
    grid_rows = BLOCKS // BR
    grid_cols = BLOCKS // BC
    covariance = covariance.reshape(BR, grid_rows, NB, ORDER).transpose(1, 0, 2, 3).reshape(ORDER, ORDER)
    covariance = covariance.reshape(ORDER, BC, grid_cols, NB).transpose(0, 2, 1, 3).reshape(ORDER, ORDER)
    return covariance


def setup_inputs(seed: int = 0) -> dict:
    keys = jax.random.split(jax.random.key(seed), 2)
    return {
        "matrix": draw_matrix(jax.random.fold_in(keys[1], 71), 0),
    }


def reference(matrix):
    grid_rows = BLOCKS // BR
    grid_cols = BLOCKS // BC
    natural = matrix.reshape(grid_rows, BR, NB, grid_cols, BC, NB).transpose(1, 0, 2, 4, 3, 5).reshape(ORDER, ORDER)
    for panel_at in range(PANELS):
        start_at = panel_at * NB
        end_at = start_at + NB
        factor = jnp.linalg.cholesky(natural[start_at:end_at, start_at:end_at])
        solved = jax.scipy.linalg.solve_triangular(factor, natural[end_at:, start_at:end_at].T, lower=True).T
        trailing = natural[end_at:, end_at:] - jnp.dot(solved.astype(jnp.float32), solved.T.astype(jnp.float32), precision=lax.Precision.HIGHEST, preferred_element_type=jnp.float32)
        natural = natural.at[start_at:end_at, start_at:end_at].set(factor)
        natural = natural.at[end_at:, start_at:end_at].set(solved)
        natural = natural.at[end_at:, end_at:].set(trailing)
    block_ids = jnp.arange(ORDER, dtype=jnp.int32) // NB
    zero_mask = (block_ids[:, None] < block_ids[None, :]) & (block_ids[:, None] < PANELS)
    natural = jnp.where(zero_mask, jnp.zeros((), jnp.float32), natural)
    return natural.reshape(BR, grid_rows, NB, BC, grid_cols, NB).transpose(1, 0, 2, 4, 3, 5).reshape(ORDER, ORDER)
```

```python
import functools

import jax
import jax.numpy as jnp
from jax import lax
from jax.experimental import pallas as pl
from jax.experimental.pallas import tpu as pltpu
from jax.sharding import PartitionSpec as P

NB = 256
PANELS = 3
HALF = 128
TILE = 8
HEAD = PANELS * NB
VMEM = 56 * 1024 * 1024

CARRIED = (((0, 0), 0), ((0, 1), 1), ((1, 2), 0), ((1, 1), 1), ((2, 0), 0), ((2, 2), 1))


def sublane(x, k):
    return jnp.broadcast_to(x[k : k + 1, :], x.shape)


def lane(x, k):
    return jnp.broadcast_to(x[:, k : k + 1], x.shape)


def dot_nt(a, b):
    return lax.dot_general(
        a, b, (((1,), (1,)), ((), ())), precision=lax.Precision.HIGHEST, preferred_element_type=jnp.float32
    )


def dot_nn(a, b):
    return jnp.dot(a, b, precision=lax.Precision.HIGHEST, preferred_element_type=jnp.float32)


def invert_factor(tiles):
    count = len(tiles)
    rows = lax.broadcasted_iota(jnp.int32, (TILE, HALF), 0)
    lanes = lax.broadcasted_iota(jnp.int32, (TILE, HALF), 1)
    out = []
    for step in range(count):
        start = TILE * step
        own = (lanes >= start) & (lanes < start + TILE)
        pivot_rows = tiles[step]
        column = [lane(pivot_rows, start + k) for k in range(TILE)]
        pivot_rows = jnp.where(own, jnp.where(lanes - start == rows, 1.0, 0.0), pivot_rows)
        upper, inverse, pivot_row, pivots = {}, [], [], None
        for k in range(TILE):
            pivot = sublane(column[k], k)
            inverse.append(pl.reciprocal(pivot, approx=False))
            pivots = pivot if pivots is None else jnp.where(rows == k, pivot, pivots)
            pivot_row.append(sublane(pivot_rows, k))
            if k < TILE - 1:
                multiplier = jnp.where(rows > k, column[k], 0.0) * inverse[k]
                for j in range(k + 1, TILE):
                    upper[k, j] = sublane(column[j], k)
                    column[j] = column[j] - multiplier * upper[k, j]
                pivot_rows = pivot_rows - multiplier * pivot_row[k]
        out.append(pivot_rows * lax.rsqrt(pivots))
        for t in range(step + 1, count):
            tile = tiles[t]
            ahead = [lane(tile, start + k) for k in range(TILE)]
            tile = jnp.where(own, 0.0, tile)
            for k in range(TILE):
                multiplier = ahead[k] * inverse[k]
                for j in range(k + 1, TILE):
                    ahead[j] = ahead[j] - multiplier * upper[k, j]
                tile = tile - multiplier * pivot_row[k]
            tiles[t] = tile
    return out


def head_kernel(core_ref, mine_ref, other_ref, inverse_ref, lower_ref, work, inverses):
    core = core_ref[0]
    halves = HEAD // HALF
    held = {}
    for (i, j), carrier in CARRIED:
        held[i, j] = jnp.where(core == carrier, mine_ref[i], other_ref[i])
    for (i, j), block in held.items():
        if j > i:
            i, j, block = j, i, block.T
        work[i * NB : (i + 1) * NB, j * NB : (j + 1) * NB] = block
    low = lax.broadcasted_iota(jnp.int32, (HALF, HALF), 0) >= lax.broadcasted_iota(jnp.int32, (HALF, HALF), 1)

    @pl.loop(0, halves)
    def _(at):
        here = pl.ds(pl.multiple_of(at * HALF, HALF), HALF)
        tiles = [work[pl.ds(pl.multiple_of(at * HALF + TILE * i, TILE), TILE), here] for i in range(HALF // TILE)]
        inverse = jnp.where(low, jnp.concatenate(invert_factor(tiles), axis=0), 0.0)
        inverses[at] = inverse
        for step in range(halves - 1):

            @pl.when(at == step)
            def _():
                after = (step + 1) * HALF
                panel = dot_nt(work[after:, step * HALF : after], inverse)
                work[after:, step * HALF : after] = panel
                for begin in range(after, HEAD, HALF):
                    end = begin + HALF
                    part = panel[begin - after :]
                    work[begin:, begin:end] = work[begin:, begin:end] - dot_nt(part, part[:HALF])

    for k in range(PANELS):
        first, second = inverses[2 * k], inverses[2 * k + 1]
        below = work[k * NB + HALF : (k + 1) * NB, k * NB : k * NB + HALF]
        inverse_ref[k, :HALF, :HALF] = first
        inverse_ref[k, :HALF, HALF:] = jnp.zeros((HALF, HALF), jnp.float32)
        inverse_ref[k, HALF:, :HALF] = -dot_nn(second, dot_nn(below, first))
        inverse_ref[k, HALF:, HALF:] = second
    lower_ref[0] = work[NB : 2 * NB, :NB]
    lower_ref[1] = work[2 * NB :, :NB]
    lower_ref[2] = work[2 * NB :, NB : 2 * NB]


def factor_head(core, mine, other):
    return pl.pallas_call(
        head_kernel,
        out_shape=[jax.ShapeDtypeStruct((PANELS, NB, NB), jnp.float32)] * 2,
        in_specs=[pl.BlockSpec(memory_space=pltpu.SMEM)] + [pl.BlockSpec(memory_space=pltpu.VMEM)] * 2,
        out_specs=[pl.BlockSpec(memory_space=pltpu.VMEM)] * 2,
        scratch_shapes=[
            pltpu.VMEM((HEAD, HEAD), jnp.float32),
            pltpu.VMEM((HEAD // HALF, HALF, HALF), jnp.float32),
        ],
        cost_estimate=pl.CostEstimate(flops=40_000_000_000, bytes_accessed=3_000_000, transcendentals=0),
        compiler_params=pltpu.CompilerParams(vmem_limit_bytes=VMEM),
        name="factor_head",
    )(core, mine, other)


def update_kernel(grid_rows, grid_cols, place_ref, inverse_ref, lower_ref, matrix_ref, *refs):
    heads, (mine_ref, other_ref, last_ref, out_ref, across) = refs[:grid_rows], refs[grid_rows:]
    my_row, my_col = place_ref[0], place_ref[1]
    core = my_col % 2
    row_slots, col_slots = matrix_ref.shape[0] // NB, matrix_ref.shape[1] // NB
    for j in range(PANELS):
        raw = heads[0][...]
        for d in range(1, grid_rows):
            raw = jnp.where((my_row ^ j) == d, heads[d][...], raw)
        if j >= 1:
            raw = raw - dot_nn(lower_ref[j - 1], across[:NB])
        if j == 2:
            raw = raw - dot_nn(lower_ref[2], across[NB : 2 * NB])
        across[j * NB : (j + 1) * NB] = dot_nn(inverse_ref[j], raw)
    low = lax.broadcasted_iota(jnp.int32, (NB, NB), 0) >= lax.broadcasted_iota(jnp.int32, (NB, NB), 1)

    @pl.loop(0, row_slots)
    def _(slot):
        here = pl.ds(pl.multiple_of(slot * NB, NB), NB)
        row = my_row + grid_rows * slot
        mine, other, last = mine_ref[here], other_ref[here], last_ref[here]
        first = dot_nt(jnp.where(core == 0, mine, other), inverse_ref[0])
        second = dot_nt(jnp.where(core == 0, other, mine) - dot_nt(first, lower_ref[0]), inverse_ref[1])
        third = dot_nt(last - dot_nt(first, lower_ref[1]) - dot_nt(second, lower_ref[2]), inverse_ref[2])
        solved = jnp.concatenate([first, second, third], axis=1)
        for t in range(col_slots):
            there = slice(t * NB, (t + 1) * NB)
            updated = matrix_ref[here, there] - dot_nn(solved, across[:, there])
            updated = jnp.where(row < PANELS, 0.0, updated)
            if t == 0:
                panel = jnp.where(my_col == 0, first, jnp.where(my_col == 1, second, third))
                panel = jnp.where((row > my_col) | ((row == my_col) & low), panel, 0.0)
                updated = jnp.where(my_col < PANELS, panel, updated)
            out_ref[here, there] = updated


def update(place, inverse, lower, matrix, heads, mine, other, last):
    grid_rows, grid_cols = lax.axis_size("row"), lax.axis_size("col")
    return pl.pallas_call(
        functools.partial(update_kernel, grid_rows, grid_cols),
        out_shape=jax.ShapeDtypeStruct(matrix.shape, jnp.float32),
        in_specs=[pl.BlockSpec(memory_space=pltpu.SMEM)]
        + [pl.BlockSpec(memory_space=pltpu.VMEM)] * (6 + len(heads)),
        out_specs=pl.BlockSpec(memory_space=pltpu.VMEM),
        scratch_shapes=[pltpu.VMEM((HEAD, matrix.shape[1]), jnp.float32)],
        cost_estimate=pl.CostEstimate(flops=10_000_000_000, bytes_accessed=10_000_000, transcendentals=0),
        compiler_params=pltpu.CompilerParams(vmem_limit_bytes=VMEM),
        name="update",
    )(place, inverse, lower, matrix, *heads, mine, other, last)


def body(matrix):
    grid_rows, grid_cols = lax.axis_size("row"), lax.axis_size("col")
    planes = grid_cols // 2
    my_row, my_col = lax.axis_index("row"), lax.axis_index("col")
    plane, core = my_col // 2, my_col % 2

    def send(x, pairs):
        flat = [(a * grid_cols + b, c * grid_cols + d) for (a, b), (c, d) in pairs]
        return lax.ppermute(x, ("row", "col"), flat)

    def swap_cores(x):
        return send(x, [((r, c), (r, c ^ 1)) for r in range(grid_rows) for c in range(grid_cols)])

    def along_rows(x):
        out = [x]
        for d in range(1, grid_rows):
            out.append(
                send(x, [((i, c), (i ^ d, c)) for i in range(PANELS) if i ^ d < grid_rows for c in range(grid_cols)])
            )
        return out

    corner = matrix[:NB, :NB]
    carried = jnp.zeros_like(corner)
    for d in [*range(1, planes), 0]:
        pairs = []
        for (i, j), carrier in CARRIED:
            target = 2 * ((j // 2 + d) % planes) + carrier
            if target != j:
                pairs.append(((i, j), (i, target)))
        carried = carried + send(corner, pairs)
    native = jnp.zeros((), jnp.bool_)
    for (i, j), carrier in CARRIED:
        if j % 2 == carrier:
            native = native | ((my_row == i) & (my_col == j))
    carried = jnp.where(native, corner, carried)
    found = along_rows(carried)
    ordered = []
    for j in range(PANELS):
        block = found[0]
        for d in range(1, grid_rows):
            block = jnp.where((my_row ^ j) == d, found[d], block)
        ordered.append(block)
    ordered = jnp.stack(ordered)
    other_ordered = swap_cores(ordered)

    strip, matrix_after, _ = lax.optimization_barrier((matrix[:, :NB], matrix, carried))
    mine, last = strip, strip
    for d in range(1, planes):
        pairs = []
        for r in range(grid_rows):
            pairs += [((r, q), (r, 2 * d + q)) for q in range(2)]
            pairs.append(((r, 2), (r, 2 * ((1 + d) % planes))))
        got = send(strip, pairs)
        mine = jnp.where(plane == d, got, mine)
        last = jnp.where((plane - 1) % planes == d, got, last)
    heads = along_rows(matrix_after[:NB])
    other, other_last = swap_cores(mine), swap_cores(last)
    last = jnp.where(core == 0, last, other_last)

    inverse, lower = factor_head(jnp.full((1,), core, jnp.int32), ordered, other_ordered)
    place = jnp.stack([my_row, my_col]).astype(jnp.int32)
    return update(place, inverse, lower, matrix, heads, mine, other, last)


def solution(mesh):
    return jax.shard_map(body, mesh=mesh, in_specs=(P("row", "col"),), out_specs=P("row", "col"), check_vma=False)
```

```python
import functools

import jax
import jax.numpy as jnp
from jax import lax
from jax.experimental import pallas as pl
from jax.experimental.pallas import tpu as pltpu
from jax.sharding import PartitionSpec as P

NB = 256
PANELS = 3
HALF = 128
TILE = 8
STEP = 16
HEAD = PANELS * NB
MIB = 1024 * 1024

CARRIED = (((0, 0), 0), ((0, 1), 1), ((1, 2), 0), ((1, 1), 1), ((2, 0), 0), ((2, 2), 1))


def sublane(x, k):
    return jnp.broadcast_to(x[k : k + 1, :], x.shape)


def lane(x, k):
    return jnp.broadcast_to(x[:, k : k + 1], x.shape)


def dot_nt(a, b):
    return lax.dot_general(
        a, b, (((1,), (1,)), ((), ())), precision=lax.Precision.HIGHEST, preferred_element_type=jnp.float32
    )


def dot_nn(a, b):
    return jnp.dot(a, b, precision=lax.Precision.HIGHEST, preferred_element_type=jnp.float32)


def opaque(x):
    return jnp.maximum(x, -3.0e38)


def total(terms):
    while len(terms) > 1:
        terms = [sum(terms[i : i + 2][1:], terms[i]) for i in range(0, len(terms), 2)]
    return terms[0]


def invert_factor(tiles):
    count, wide = len(tiles), STEP // TILE
    rows = lax.broadcasted_iota(jnp.int32, (TILE, HALF), 0)
    lanes = lax.broadcasted_iota(jnp.int32, (TILE, HALF), 1)
    out = []
    for step in range(0, count, wide):
        start, after = TILE * step, step + wide
        own = (lanes >= start) & (lanes < start + STEP)
        column = [[opaque(lane(tiles[step + e], start + k)) for e in range(wide)] for k in range(STEP)]
        forward = [
            jnp.where(own, jnp.where(lanes - start == rows + TILE * e, 1.0, 0.0), tiles[step + e]) for e in range(wide)
        ]
        solved, pivots, below = list(forward), [], {}
        for k in range(0, STEP, 2):
            o, i = k // TILE, k % TILE
            a, b, c = sublane(column[k][o], i), sublane(column[k + 1][o], i), sublane(column[k + 1][o], i + 1)
            det = a * c - b * b
            inverse = pl.reciprocal(det, approx=False)
            pivots.append((a, b, c, det, inverse))
            if k == 0:
                zero = jnp.minimum(jnp.abs(inverse), 0.0)
                for t in range(after, count):
                    below[t] = [lane(tiles[t] + zero, start + j) for j in range(STEP)]
            one = [column[k][e] * c - column[k + 1][e] * b for e in range(wide)]
            two = [column[k + 1][e] * a - column[k][e] * b for e in range(wide)]
            pair = (rows == i) | (rows == i + 1)
            one[o], two[o] = jnp.where(pair, 0.0, one[o]), jnp.where(pair, 0.0, two[o])
            first, second = [x * inverse for x in one], [x * inverse for x in two]
            for j in range(k + 2, STEP):
                u, v = sublane(column[j][o], i), sublane(column[j][o], i + 1)
                for e in range(wide):
                    if j < k + 4:
                        column[j][e] = column[j][e] - (one[e] * u + two[e] * v) * inverse
                    else:
                        column[j][e] = column[j][e] - (first[e] * u + second[e] * v)
            u, v = sublane(forward[o], i), sublane(forward[o], i + 1)
            x, y = sublane(solved[o], i), sublane(solved[o], i + 1)
            for e in range(wide):
                if after < count:
                    solved[e] = solved[e] - (first[e] * x + second[e] * y)
                if e > o:
                    forward[e] = forward[e] - (first[e] * u + second[e] * v)
                elif e == o and i + 2 < TILE:
                    forward[e] = forward[e] - jnp.where(rows > i, first[e] * u + second[e] * v, 0.0)
        if after < count:
            right = []
            for k in range(0, STEP, 2):
                o, i = k // TILE, k % TILE
                a, b, c, _, inverse = pivots[k // 2]
                x, y = sublane(solved[o], i), sublane(solved[o], i + 1)
                right += [(x * c - y * b) * inverse, (y * a - x * b) * inverse]
            for t in range(after, count):
                tiles[t] = jnp.where(own, 0.0, tiles[t]) - total([below[t][k] * right[k] for k in range(STEP)])
        for e in range(wide):
            diagonal, within = jnp.ones_like(forward[e]), jnp.zeros_like(forward[e])
            for i in range(0, TILE, 2):
                a, b, _, det, _ = pivots[(TILE * e + i) // 2]
                inverse = pl.reciprocal(a, approx=False)
                diagonal = jnp.where(rows == i, a, jnp.where(rows == i + 1, det * inverse, diagonal))
                within = jnp.where(rows == i + 1, b * inverse * sublane(forward[e], i), within)
            out.append((forward[e] - within) * lax.rsqrt(diagonal))
    return out


def assemble(my_row, core, found, mirrored, work):
    for (i, j), carrier in CARRIED:
        for d in range(len(found)):

            @pl.when((my_row ^ i) == d)
            def _():
                block = jnp.where(core == carrier, found[d][...], mirrored[d][...])
                if j > i:
                    work[j * NB : (j + 1) * NB, i * NB : (i + 1) * NB] = block.T
                else:
                    work[i * NB : (i + 1) * NB, j * NB : (j + 1) * NB] = block


def head_kernel(begin, end, place_ref, *refs):
    inverse_ref, work = refs[-2:]
    if begin == 0:
        count = (len(refs) - 2) // 2
        assemble(place_ref[0], place_ref[1] % 2, refs[:count], refs[count : 2 * count], work)
    else:
        work[...] = refs[0][...]
    low = lax.broadcasted_iota(jnp.int32, (HALF, HALF), 0) >= lax.broadcasted_iota(jnp.int32, (HALF, HALF), 1)

    @pl.loop(2 * begin, 2 * end)
    def _(at):
        here = pl.ds(pl.multiple_of(at * HALF, HALF), HALF)
        tiles = [work[pl.ds(pl.multiple_of(at * HALF + TILE * i, TILE), TILE), here] for i in range(HALF // TILE)]
        inverse = jnp.where(low, jnp.concatenate(invert_factor(tiles), axis=0), 0.0)
        diagonal = pl.ds(pl.multiple_of((at % 2) * HALF, HALF), HALF)
        inverse_ref[at // 2 - begin, diagonal, diagonal] = inverse
        work[here, here] = jnp.where(low, dot_nt(work[here, here], inverse), 0.0)
        for step in range(2 * begin, min(2 * end, HEAD // HALF - 1)):

            @pl.when(at == step)
            def _():
                after = (step + 1) * HALF
                solved = dot_nt(work[after:, step * HALF : after], inverse)
                work[after:, step * HALF : after] = solved
                for left in range(after, HEAD, HALF):
                    right = left + HALF
                    part = solved[left - after :]
                    work[left:, left:right] = work[left:, left:right] - dot_nt(part, part[:HALF])

    for k in range(begin, end):
        first, second = inverse_ref[k - begin, :HALF, :HALF], inverse_ref[k - begin, HALF:, HALF:]
        below = work[k * NB + HALF : (k + 1) * NB, k * NB : k * NB + HALF]
        inverse_ref[k - begin, HALF:, :HALF] = -dot_nn(second, dot_nn(below, first))
        inverse_ref[k - begin, :HALF, HALF:] = jnp.zeros((HALF, HALF), jnp.float32)
        work[k * NB : k * NB + HALF, k * NB + HALF : (k + 1) * NB] = jnp.zeros((HALF, HALF), jnp.float32)


def factor_panels(begin, end, place, *blocks):
    return pl.pallas_call(
        functools.partial(head_kernel, begin, end),
        out_shape=[
            jax.ShapeDtypeStruct((end - begin, NB, NB), jnp.float32),
            jax.ShapeDtypeStruct((HEAD, HEAD), jnp.float32),
        ],
        in_specs=[pl.BlockSpec(memory_space=pltpu.SMEM)] + [pl.BlockSpec(memory_space=pltpu.VMEM)] * len(blocks),
        out_specs=[pl.BlockSpec(memory_space=pltpu.VMEM)] * 2,
        cost_estimate=pl.CostEstimate(flops=1_000, bytes_accessed=1_000, transcendentals=0),
        compiler_params=pltpu.CompilerParams(vmem_limit_bytes=(14 if begin else 56) * MIB),
        name="factor_panels",
    )(place, *blocks)


def update_kernel(grid_rows, place_ref, early_ref, late_ref, head_ref, top_ref, top_other_ref, *refs):
    (held_ref, held_other_ref, swapped_ref, swapped_other_ref), heads = refs[:4], refs[4:-4]
    matrix_ref, out_ref, across, solved = refs[-4:]
    my_row, my_col = place_ref[0], place_ref[1]
    plane, core = my_col // 2, my_col % 2
    slot = pl.program_id(0)
    row = my_row + grid_rows * slot
    col_slots = out_ref.shape[1] // NB
    inverse = (early_ref.at[0], late_ref.at[0], late_ref.at[1])
    lower = {
        (i, j): head_ref.at[i * NB : (i + 1) * NB, j * NB : (j + 1) * NB] for i, j in ((1, 0), (2, 0), (2, 1))
    }

    @pl.when(slot == 0)
    def _():
        for j in range(PANELS):
            raw = heads[0][...]
            for d in range(1, grid_rows):
                raw = jnp.where((my_row ^ j) == d, heads[d][...], raw)
            for i in range(j):
                raw = raw - dot_nn(lower[j, i][...], across[i * NB : (i + 1) * NB])
            across[j * NB : (j + 1) * NB] = dot_nn(inverse[j][...], raw)

        def by_core(mine, other):
            return jnp.where(core == 0, mine, other)

        held, held_other = held_ref[...], held_other_ref[...]
        swapped, swapped_other = swapped_ref[...], swapped_other_ref[...]
        even = plane % 2 == 0
        own, across_core = jnp.where(even, held, swapped), jnp.where(even, held_other, swapped_other)
        last = jnp.where(even, by_core(swapped, swapped_other), by_core(held, held_other))
        first, second, third = top_ref[0], top_other_ref[0], by_core(top_ref[1], top_other_ref[1])
        raw = [
            jnp.concatenate([by_core(first, second), by_core(own, across_core)], axis=0),
            jnp.concatenate([by_core(second, first), by_core(across_core, own)], axis=0),
            jnp.concatenate([third, last], axis=0),
        ]
        for j in range(PANELS):
            rest = raw[j]
            for i in range(j):
                rest = rest - dot_nt(solved[:, i * NB : (i + 1) * NB], lower[j, i][...])
            solved[:, j * NB : (j + 1) * NB] = dot_nt(rest, inverse[j][...])

    mine = solved[pl.ds(pl.multiple_of(slot * NB, NB), NB), :]
    head_row = pl.ds(pl.multiple_of(jnp.minimum(my_row, PANELS - 1) * NB, NB), NB)
    head_col = pl.ds(pl.multiple_of(jnp.minimum(my_col, PANELS - 1) * NB, NB), NB)
    for t in range(col_slots):
        there = slice(t * NB, (t + 1) * NB)
        updated = matrix_ref[:, there] - dot_nn(mine, across[:, there])
        updated = jnp.where(row < PANELS, 0.0, updated)
        if t == 0:
            panel = mine[:, :NB]
            for j in range(1, PANELS):
                panel = jnp.where(my_col == j, mine[:, j * NB : (j + 1) * NB], panel)
            factor = jnp.where(my_col <= row, head_ref[head_row, head_col], 0.0)
            panel = jnp.where(row < PANELS, factor, panel)
            updated = jnp.where(my_col < PANELS, panel, updated)
        out_ref[:, there] = updated


def update(place, early, late, head, top, top_other, sent, heads, matrix):
    whole = pl.BlockSpec(memory_space=pltpu.VMEM)
    strip = pl.BlockSpec((NB, matrix.shape[1]), lambda slot: (slot, 0))
    return pl.pallas_call(
        functools.partial(update_kernel, len(heads)),
        out_shape=jax.ShapeDtypeStruct(matrix.shape, jnp.float32),
        grid=(matrix.shape[0] // NB,),
        in_specs=[pl.BlockSpec(memory_space=pltpu.SMEM)] + [whole] * (5 + len(sent) + len(heads)) + [strip],
        out_specs=strip,
        scratch_shapes=[
            pltpu.VMEM((HEAD, matrix.shape[1]), jnp.float32),
            pltpu.VMEM((matrix.shape[0], HEAD), jnp.float32),
        ],
        cost_estimate=pl.CostEstimate(flops=10_000_000_000, bytes_accessed=10_000_000, transcendentals=0),
        compiler_params=pltpu.CompilerParams(vmem_limit_bytes=(30 if len(heads) <= 4 else 56) * MIB),
        name="update",
    )(place, early, late, head, top, top_other, *sent, *heads, matrix)


def body(matrix):
    grid_rows, grid_cols = lax.axis_size("row"), lax.axis_size("col")
    planes = grid_cols // 2
    my_row, my_col = lax.axis_index("row"), lax.axis_index("col")
    plane, core = my_col // 2, my_col % 2

    def send(x, pairs):
        flat = [(a * grid_cols + b, c * grid_cols + d) for (a, b), (c, d) in pairs]
        return lax.ppermute(x, ("row", "col"), flat)

    def swap_cores(x):
        return send(x, [((r, c), (r, c ^ 1)) for r in range(grid_rows) for c in range(grid_cols)])

    def along_rows(x):
        out = [x]
        for d in range(1, grid_rows):
            out.append(
                send(x, [((i, c), (i ^ d, c)) for i in range(PANELS) if i ^ d < grid_rows for c in range(grid_cols)])
            )
        return out

    place = jnp.stack([my_row, my_col]).astype(jnp.int32)
    corner = matrix[:NB, :NB]
    carried = jnp.zeros_like(corner)
    passed = []
    for d in [*range(1, planes), 0]:
        pairs = []
        for (i, j), carrier in CARRIED:
            target = 2 * ((j // 2 + d) % planes) + carrier
            if target != j:
                pairs.append(((i, j), (i, target)))
        if d:
            for r in range(PANELS, grid_rows):
                pairs += [((r, q), (r, 2 * d + q)) for q in range(2)]
                pairs.append(((r, 2), (r, 2 * ((1 + d) % planes))))
        passed.append(send(corner, pairs))
        carried = carried + passed[-1]
    native = jnp.zeros((), jnp.bool_)
    for (i, j), carrier in CARRIED:
        if j % 2 == carrier:
            native = native | ((my_row == i) & (my_col == j))
    carried = jnp.where(native, corner, carried)
    heads = along_rows(matrix[:NB])
    found = along_rows(carried)
    top_mine, top_last = corner, corner
    for d in range(1, planes):
        top_mine = jnp.where(plane == d, passed[d - 1], top_mine)
        top_last = jnp.where((plane - 1) % planes == d, passed[d - 1], top_last)
    found, top = lax.optimization_barrier((found, jnp.stack([top_mine, top_last])))
    mirrored = [swap_cores(x) for x in found]
    strip, _ = lax.optimization_barrier((matrix[NB:, :NB], carried))

    held = strip
    distance = planes // 2
    while distance > 1:
        pairs = []
        for z in range(0, planes, 2 * distance):
            for r in range(grid_rows):
                pairs += [((r, 2 * z + q), (r, 2 * (z + distance) + q)) for q in range(2)]
                pairs.append(((r, 2 * z + 2), (r, 2 * (z + distance) + 2)))
        got = send(held, pairs)
        if distance == 2:
            early, head = factor_panels(0, 1, place, *found, *mirrored)
            got, head, heads = lax.optimization_barrier((got, head, heads))
        held = jnp.where((plane // distance) % 2 == 1, got, held)
        distance //= 2
    held, head, top = lax.optimization_barrier((held, head, top))
    pairs = []
    for z in range(0, planes, 2):
        for r in range(grid_rows):
            pairs += [((r, 2 * z + q), (r, 2 * z + 2 + q)) for q in range(2)]
            pairs.append(((r, 2 * z + 2), (r, 2 * z)))
    swapped = send(held, pairs)
    held_other, top_other = swap_cores(held), swap_cores(top)
    late, head = factor_panels(1, PANELS, place, head)
    swapped, late, head = lax.optimization_barrier((swapped, late, head))
    sent = [held, held_other, swapped, swap_cores(swapped)]
    return update(place, early, late, head, top, top_other, sent, heads, matrix)


def solution(mesh):
    return jax.shard_map(body, mesh=mesh, in_specs=(P("row", "col"),), out_specs=P("row", "col"), check_vma=False)
```

```python
import functools

import jax
import jax.numpy as jnp
from jax import lax
from jax.experimental import pallas as pl
from jax.experimental.pallas import tpu as pltpu
from jax.sharding import PartitionSpec as P

NB = 256
PANELS = 3
HALF = 128
TILE = 8
STEP = 16
EARLY = 3
HEAD = PANELS * NB
MIB = 1024 * 1024

CARRIED = (((0, 0), 0), ((0, 1), 1), ((1, 2), 0), ((1, 1), 1), ((2, 0), 0), ((2, 2), 1))


def sublane(x, k):
    return jnp.broadcast_to(x[k : k + 1, :], x.shape)


def lane(x, k):
    return jnp.broadcast_to(x[:, k : k + 1], x.shape)


def dot_nt(a, b):
    return lax.dot_general(
        a, b, (((1,), (1,)), ((), ())), precision=lax.Precision.HIGHEST, preferred_element_type=jnp.float32
    )


def dot_nn(a, b):
    return jnp.dot(a, b, precision=lax.Precision.HIGHEST, preferred_element_type=jnp.float32)


def opaque(x):
    return jnp.maximum(x, -3.0e38)


def total(terms):
    while len(terms) > 1:
        terms = [sum(terms[i : i + 2][1:], terms[i]) for i in range(0, len(terms), 2)]
    return terms[0]


def invert_factor(tiles):
    count, wide = len(tiles), STEP // TILE
    rows = lax.broadcasted_iota(jnp.int32, (TILE, HALF), 0)
    lanes = lax.broadcasted_iota(jnp.int32, (TILE, HALF), 1)
    out = []
    for step in range(0, count, wide):
        start, after = TILE * step, step + wide
        own = (lanes >= start) & (lanes < start + STEP)
        column = [[opaque(lane(tiles[step + e], start + k)) for e in range(wide)] for k in range(STEP)]
        forward = [
            jnp.where(own, jnp.where(lanes - start == rows + TILE * e, 1.0, 0.0), tiles[step + e]) for e in range(wide)
        ]
        solved, pivots, below = list(forward), [], {}
        for k in range(0, STEP, 2):
            o, i = k // TILE, k % TILE
            a, b, c = sublane(column[k][o], i), sublane(column[k + 1][o], i), sublane(column[k + 1][o], i + 1)
            det = a * c - b * b
            inverse = pl.reciprocal(det, approx=False)
            pivots.append((a, b, c, det, inverse))
            if k == 0:
                zero = jnp.minimum(jnp.abs(inverse), 0.0)
                for t in range(after, min(after + wide, count)):
                    below[t] = [lane(tiles[t] + zero, start + j) for j in range(STEP)]
            one = [column[k][e] * c - column[k + 1][e] * b for e in range(wide)]
            two = [column[k + 1][e] * a - column[k][e] * b for e in range(wide)]
            pair = (rows == i) | (rows == i + 1)
            one[o], two[o] = jnp.where(pair, 0.0, one[o]), jnp.where(pair, 0.0, two[o])
            first, second = [x * inverse for x in one], [x * inverse for x in two]
            for j in range(k + 2, STEP):
                u, v = sublane(column[j][o], i), sublane(column[j][o], i + 1)
                for e in range(wide):
                    if j < k + 4:
                        column[j][e] = column[j][e] - (one[e] * u + two[e] * v) * inverse
                    else:
                        column[j][e] = column[j][e] - (first[e] * u + second[e] * v)
            u, v = sublane(forward[o], i), sublane(forward[o], i + 1)
            x, y = sublane(solved[o], i), sublane(solved[o], i + 1)
            for e in range(wide):
                if after < count:
                    solved[e] = solved[e] - (first[e] * x + second[e] * y)
                if e > o:
                    forward[e] = forward[e] - (first[e] * u + second[e] * v)
                elif e == o and i + 2 < TILE:
                    forward[e] = forward[e] - jnp.where(rows > i, first[e] * u + second[e] * v, 0.0)
        if after < count:
            right = []
            for k in range(0, STEP, 2):
                o, i = k // TILE, k % TILE
                a, b, c, _, inverse = pivots[k // 2]
                x, y = sublane(solved[o], i), sublane(solved[o], i + 1)
                right += [(x * c - y * b) * inverse, (y * a - x * b) * inverse]
            for t in below:
                tiles[t] = jnp.where(own, 0.0, tiles[t]) - total([below[t][k] * right[k] for k in range(STEP)])
            far = after + wide
            if far < count:
                packed = [jnp.zeros_like(tiles[0])] * count
                for e in range(wide):
                    packed[step + e] = right[TILE * e]
                    for i in range(1, TILE):
                        packed[step + e] = jnp.where(rows == i, right[TILE * e + i], packed[step + e])
                product = dot_nn(jnp.concatenate(tiles[far:], axis=0), jnp.concatenate(packed, axis=0))
                for t in range(far, count):
                    tiles[t] = jnp.where(own, 0.0, tiles[t]) - product[TILE * (t - far) : TILE * (t - far + 1)]
        for e in range(wide):
            diagonal, within = jnp.ones_like(forward[e]), jnp.zeros_like(forward[e])
            for i in range(0, TILE, 2):
                a, b, _, det, _ = pivots[(TILE * e + i) // 2]
                inverse = pl.reciprocal(a, approx=False)
                diagonal = jnp.where(rows == i, a, jnp.where(rows == i + 1, det * inverse, diagonal))
                within = jnp.where(rows == i + 1, b * inverse * sublane(forward[e], i), within)
            out.append((forward[e] - within) * lax.rsqrt(diagonal))
    return out


def assemble(my_row, core, found, mirrored, work):
    for (i, j), carrier in CARRIED:
        for d in range(len(found)):

            @pl.when((my_row ^ i) == d)
            def _():
                block = jnp.where(core == carrier, found[d][...], mirrored[d][...])
                if j > i:
                    work[j * NB : (j + 1) * NB, i * NB : (i + 1) * NB] = block.T
                else:
                    work[i * NB : (i + 1) * NB, j * NB : (j + 1) * NB] = block


def head_kernel(begin, end, place_ref, *refs):
    inverse_ref, work = refs[-2:]
    if begin == 0:
        count = (len(refs) - 2) // 2
        assemble(place_ref[0], place_ref[1] % 2, refs[:count], refs[count : 2 * count], work)
    else:
        work[...] = refs[0][...]
    low = lax.broadcasted_iota(jnp.int32, (HALF, HALF), 0) >= lax.broadcasted_iota(jnp.int32, (HALF, HALF), 1)

    for at in range(2 * begin, 2 * end):
        left, right = at * HALF, (at + 1) * HALF
        block = work[left:right, left:right]
        tiles = [block[TILE * i : TILE * (i + 1)] for i in range(HALF // TILE)]
        inverse = jnp.where(low, jnp.concatenate(invert_factor(tiles), axis=0), 0.0)
        diagonal = slice((at % 2) * HALF, (at % 2 + 1) * HALF)
        inverse_ref[at // 2 - begin, diagonal, diagonal] = inverse
        work[left:right, left:right] = jnp.where(low, dot_nt(block, inverse), 0.0)
        if right < HEAD:
            solved = dot_nt(work[right:, left:right], inverse)
            work[right:, left:right] = solved
            for column in range(right, HEAD, HALF):
                part = solved[column - right :]
                part = work[column:, column : column + HALF] - dot_nt(part, part[:HALF])
                work[column:, column : column + HALF] = part

    for k in range(begin, end):
        first, second = inverse_ref[k - begin, :HALF, :HALF], inverse_ref[k - begin, HALF:, HALF:]
        below = work[k * NB + HALF : (k + 1) * NB, k * NB : k * NB + HALF]
        inverse_ref[k - begin, HALF:, :HALF] = -dot_nn(second, dot_nn(below, first))
        inverse_ref[k - begin, :HALF, HALF:] = jnp.zeros((HALF, HALF), jnp.float32)
        work[k * NB : k * NB + HALF, k * NB + HALF : (k + 1) * NB] = jnp.zeros((HALF, HALF), jnp.float32)


def factor_panels(begin, end, place, *blocks):
    return pl.pallas_call(
        functools.partial(head_kernel, begin, end),
        out_shape=[
            jax.ShapeDtypeStruct((end - begin, NB, NB), jnp.float32),
            jax.ShapeDtypeStruct((HEAD, HEAD), jnp.float32),
        ],
        in_specs=[pl.BlockSpec(memory_space=pltpu.SMEM)] + [pl.BlockSpec(memory_space=pltpu.VMEM)] * len(blocks),
        out_specs=[pl.BlockSpec(memory_space=pltpu.VMEM)] * 2,
        cost_estimate=pl.CostEstimate(flops=1_000, bytes_accessed=1_000, transcendentals=0),
        compiler_params=pltpu.CompilerParams(vmem_limit_bytes=(14 if begin else 56) * MIB),
        name="factor_panels",
    )(place, *blocks)


def across_kernel(place_ref, early_ref, late_ref, head_ref, *refs):
    heads, across = refs[:-1], refs[-1]
    inverse, lower = head_blocks(early_ref, late_ref, head_ref)
    for j in range(PANELS):
        raw = heads[0][...]
        for d in range(1, len(heads)):
            raw = jnp.where((place_ref[0] ^ j) == d, heads[d][...], raw)
        for i in range(j):
            raw = raw - dot_nn(lower[j, i][...], across[i * NB : (i + 1) * NB])
        across[j * NB : (j + 1) * NB] = dot_nn(inverse[j][...], raw)


def head_blocks(early_ref, late_ref, head_ref):
    inverse = (early_ref.at[0], late_ref.at[0], late_ref.at[1])
    lower = {
        (i, j): head_ref.at[i * NB : (i + 1) * NB, j * NB : (j + 1) * NB] for i, j in ((1, 0), (2, 0), (2, 1))
    }
    return inverse, lower


def solve_across(place, early, late, head, heads):
    whole = pl.BlockSpec(memory_space=pltpu.VMEM)
    return pl.pallas_call(
        across_kernel,
        out_shape=jax.ShapeDtypeStruct((HEAD, heads[0].shape[1]), jnp.float32),
        in_specs=[pl.BlockSpec(memory_space=pltpu.SMEM)] + [whole] * (3 + len(heads)),
        out_specs=whole,
        cost_estimate=pl.CostEstimate(flops=4_000_000_000, bytes_accessed=5_000_000, transcendentals=0),
        compiler_params=pltpu.CompilerParams(vmem_limit_bytes=(20 if len(heads) <= 4 else 56) * MIB),
        name="solve_across",
    )(place, early, late, head, *heads)


def update_kernel(grid_rows, place_ref, early_ref, late_ref, head_ref, top_ref, top_other_ref, *refs):
    held_ref, held_other_ref, swapped_ref, swapped_other_ref, across, matrix_ref, out_ref, solved = refs
    my_row, my_col = place_ref[0], place_ref[1]
    plane, core = my_col // 2, my_col % 2
    step = pl.program_id(0)
    inverse, lower = head_blocks(early_ref, late_ref, head_ref)

    @pl.when(step == 0)
    def _():
        def by_core(mine, other):
            return jnp.where(core == 0, mine, other)

        held, held_other = held_ref[...], held_other_ref[...]
        swapped, swapped_other = swapped_ref[...], swapped_other_ref[...]
        even = plane % 2 == 0
        own, across_core = jnp.where(even, held, swapped), jnp.where(even, held_other, swapped_other)
        last = jnp.where(even, by_core(swapped, swapped_other), by_core(held, held_other))
        first, second, third = top_ref[0], top_other_ref[0], by_core(top_ref[1], top_other_ref[1])
        raw = [
            jnp.concatenate([by_core(first, second), by_core(own, across_core)], axis=0),
            jnp.concatenate([by_core(second, first), by_core(across_core, own)], axis=0),
            jnp.concatenate([third, last], axis=0),
        ]
        depth = solved.shape[0] // 2
        for j in range(PANELS):
            there = slice(j * NB, (j + 1) * NB)
            for here in (slice(0, depth), slice(depth, 2 * depth)):
                rest = raw[j][here]
                for i in range(j):
                    rest = rest - dot_nt(solved[here, i * NB : (i + 1) * NB], lower[j, i][...])
                solved[here, there] = dot_nt(rest, inverse[j][...])

    depth = out_ref.shape[0]
    product = dot_nn(solved[pl.ds(pl.multiple_of(step * depth, depth), depth), :], across[...])
    head_row = pl.ds(pl.multiple_of(jnp.minimum(my_row, PANELS - 1) * NB, NB), NB)
    head_col = pl.ds(pl.multiple_of(jnp.minimum(my_col, PANELS - 1) * NB, NB), NB)
    for block in range(depth // NB):
        slot = step * (depth // NB) + block
        row = my_row + grid_rows * slot
        here = slice(block * NB, (block + 1) * NB)
        mine = solved[pl.ds(pl.multiple_of(slot * NB, NB), NB), :]
        for t in range(out_ref.shape[1] // NB):
            there = slice(t * NB, (t + 1) * NB)
            updated = matrix_ref[here, there] - product[here, there]
            updated = jnp.where(row < PANELS, 0.0, updated)
            if t == 0:
                panel = mine[:, :NB]
                for j in range(1, PANELS):
                    panel = jnp.where(my_col == j, mine[:, j * NB : (j + 1) * NB], panel)
                factor = jnp.where(my_col <= row, head_ref[head_row, head_col], 0.0)
                panel = jnp.where(row < PANELS, factor, panel)
                updated = jnp.where(my_col < PANELS, panel, updated)
            out_ref[here, there] = updated


def update(grid_rows, place, early, late, head, top, top_other, sent, across, matrix):
    whole = pl.BlockSpec(memory_space=pltpu.VMEM)
    depth = 2 * NB if matrix.shape[0] % (2 * NB) == 0 else NB
    strip = pl.BlockSpec((depth, matrix.shape[1]), lambda step: (step, 0))
    return pl.pallas_call(
        functools.partial(update_kernel, grid_rows),
        out_shape=jax.ShapeDtypeStruct(matrix.shape, jnp.float32),
        grid=(matrix.shape[0] // depth,),
        in_specs=[pl.BlockSpec(memory_space=pltpu.SMEM)] + [whole] * (6 + len(sent)) + [strip],
        out_specs=strip,
        scratch_shapes=[pltpu.VMEM((matrix.shape[0], HEAD), jnp.float32)],
        cost_estimate=pl.CostEstimate(flops=10_000_000_000, bytes_accessed=10_000_000, transcendentals=0),
        compiler_params=pltpu.CompilerParams(vmem_limit_bytes=30 * MIB),
        name="update",
    )(place, early, late, head, top, top_other, *sent, across, matrix)


def body(matrix):
    grid_rows, grid_cols = lax.axis_size("row"), lax.axis_size("col")
    planes = grid_cols // 2
    my_row, my_col = lax.axis_index("row"), lax.axis_index("col")
    plane, core = my_col // 2, my_col % 2

    def send(x, pairs):
        flat = [(a * grid_cols + b, c * grid_cols + d) for (a, b), (c, d) in pairs]
        return lax.ppermute(x, ("row", "col"), flat)

    def swap_cores(x):
        return send(x, [((r, c), (r, c ^ 1)) for r in range(grid_rows) for c in range(grid_cols)])

    def along_rows(x):
        out = [x]
        for d in range(1, grid_rows):
            out.append(
                send(x, [((i, c), (i ^ d, c)) for i in range(PANELS) if i ^ d < grid_rows for c in range(grid_cols)])
            )
        return out

    place = jnp.stack([my_row, my_col]).astype(jnp.int32)
    corner = matrix[:NB, :NB]
    carried = jnp.zeros_like(corner)
    passed = []
    for d in [*range(1, planes), 0]:
        pairs = []
        for (i, j), carrier in CARRIED:
            target = 2 * ((j // 2 + d) % planes) + carrier
            if target != j:
                pairs.append(((i, j), (i, target)))
        if d:
            for r in range(PANELS, grid_rows):
                pairs += [((r, q), (r, 2 * d + q)) for q in range(2)]
                pairs.append(((r, 2), (r, 2 * ((1 + d) % planes))))
        passed.append(send(corner, pairs))
        carried = carried + passed[-1]
    native = jnp.zeros((), jnp.bool_)
    for (i, j), carrier in CARRIED:
        if j % 2 == carrier:
            native = native | ((my_row == i) & (my_col == j))
    carried = jnp.where(native, corner, carried)
    heads = along_rows(matrix[:NB])
    found = along_rows(carried)
    found, early_heads = lax.optimization_barrier((found, heads[:EARLY]))
    heads = [*early_heads, *heads[EARLY:]]
    top_mine, top_last = corner, corner
    for d in range(1, planes):
        top_mine = jnp.where(plane == d, passed[d - 1], top_mine)
        top_last = jnp.where((plane - 1) % planes == d, passed[d - 1], top_last)
    found, top = lax.optimization_barrier((found, jnp.stack([top_mine, top_last])))
    mirrored = [swap_cores(x) for x in found]
    strip, _ = lax.optimization_barrier((matrix[NB:, :NB], carried))

    held = strip
    distance = planes // 2
    while distance > 1:
        pairs = []
        for z in range(0, planes, 2 * distance):
            for r in range(grid_rows):
                pairs += [((r, 2 * z + q), (r, 2 * (z + distance) + q)) for q in range(2)]
                pairs.append(((r, 2 * z + 2), (r, 2 * (z + distance) + 2)))
        got = send(held, pairs)
        if distance == 2:
            early, head = factor_panels(0, 1, place, *found, *mirrored)
            got, head, heads = lax.optimization_barrier((got, head, heads))
        held = jnp.where((plane // distance) % 2 == 1, got, held)
        distance //= 2
    held, head, top = lax.optimization_barrier((held, head, top))
    pairs = []
    for z in range(0, planes, 2):
        for r in range(grid_rows):
            pairs += [((r, 2 * z + q), (r, 2 * z + 2 + q)) for q in range(2)]
            pairs.append(((r, 2 * z + 2), (r, 2 * z)))
    swapped = send(held, pairs)
    held_other, top_other = swap_cores(held), swap_cores(top)
    late, head = factor_panels(1, PANELS, place, head)
    across = solve_across(place, early, late, head, heads)
    swapped, across = lax.optimization_barrier((swapped, across))
    swapped_other = swap_cores(swapped)
    sent = [held, held_other, swapped, swapped_other]
    return update(grid_rows, place, early, late, head, top, top_other, sent, across, matrix)


def solution(mesh):
    return jax.shard_map(body, mesh=mesh, in_specs=(P("row", "col"),), out_specs=P("row", "col"), check_vma=False)
```

```python
import functools

import jax
import jax.numpy as jnp
from jax import lax
from jax.experimental import pallas as pl
from jax.experimental.pallas import tpu as pltpu
from jax.sharding import PartitionSpec as P

NB = 256
PANELS = 3
HALF = 128
TILE = 8
STEP = 16
EARLY = 3
HEAD = PANELS * NB
MIB = 1024 * 1024

CARRIED = (((0, 0), 0), ((0, 1), 1), ((1, 2), 0), ((1, 1), 1), ((2, 0), 0), ((2, 2), 1))


def sublane(x, k):
    return jnp.broadcast_to(x[k : k + 1, :], x.shape)


def lane(x, k):
    return jnp.broadcast_to(x[:, k : k + 1], x.shape)


def dot_nt(a, b):
    return lax.dot_general(
        a, b, (((1,), (1,)), ((), ())), precision=lax.Precision.HIGHEST, preferred_element_type=jnp.float32
    )


def dot_nn(a, b):
    return jnp.dot(a, b, precision=lax.Precision.HIGHEST, preferred_element_type=jnp.float32)


def opaque(x):
    return jnp.maximum(x, -3.0e38)


def total(terms):
    while len(terms) > 1:
        terms = [sum(terms[i : i + 2][1:], terms[i]) for i in range(0, len(terms), 2)]
    return terms[0]


def invert_factor(tiles):
    count, wide = len(tiles), STEP // TILE
    rows = lax.broadcasted_iota(jnp.int32, (TILE, HALF), 0)
    lanes = lax.broadcasted_iota(jnp.int32, (TILE, HALF), 1)
    out = []
    for step in range(0, count, wide):
        start, after = TILE * step, step + wide
        own = (lanes >= start) & (lanes < start + STEP)
        column = [[opaque(lane(tiles[step + e], start + k)) for e in range(wide)] for k in range(STEP)]
        forward = [
            jnp.where(own, jnp.where(lanes - start == rows + TILE * e, 1.0, 0.0), tiles[step + e]) for e in range(wide)
        ]
        solved, pivots, below = list(forward), [], {}
        for k in range(0, STEP, 2):
            o, i = k // TILE, k % TILE
            a, b, c = sublane(column[k][o], i), sublane(column[k + 1][o], i), sublane(column[k + 1][o], i + 1)
            det = a * c - b * b
            inverse = pl.reciprocal(det, approx=False)
            pivots.append((a, b, c, det, inverse))
            if k == 0:
                zero = jnp.minimum(jnp.abs(inverse), 0.0)
                for t in range(after, min(after + wide, count)):
                    below[t] = [lane(tiles[t] + zero, start + j) for j in range(STEP)]
            one = [column[k][e] * c - column[k + 1][e] * b for e in range(wide)]
            two = [column[k + 1][e] * a - column[k][e] * b for e in range(wide)]
            pair = (rows == i) | (rows == i + 1)
            one[o], two[o] = jnp.where(pair, 0.0, one[o]), jnp.where(pair, 0.0, two[o])
            first, second = [x * inverse for x in one], [x * inverse for x in two]
            for j in range(k + 2, STEP):
                u, v = sublane(column[j][o], i), sublane(column[j][o], i + 1)
                for e in range(wide):
                    if j < k + 4:
                        column[j][e] = column[j][e] - (one[e] * u + two[e] * v) * inverse
                    else:
                        column[j][e] = column[j][e] - (first[e] * u + second[e] * v)
            u, v = sublane(forward[o], i), sublane(forward[o], i + 1)
            x, y = sublane(solved[o], i), sublane(solved[o], i + 1)
            for e in range(wide):
                if after < count:
                    solved[e] = solved[e] - (first[e] * x + second[e] * y)
                if e > o:
                    forward[e] = forward[e] - (first[e] * u + second[e] * v)
                elif e == o and i + 2 < TILE:
                    forward[e] = forward[e] - jnp.where(rows > i, first[e] * u + second[e] * v, 0.0)
        if after < count:
            right = []
            for k in range(0, STEP, 2):
                o, i = k // TILE, k % TILE
                a, b, c, _, inverse = pivots[k // 2]
                x, y = sublane(solved[o], i), sublane(solved[o], i + 1)
                right += [(x * c - y * b) * inverse, (y * a - x * b) * inverse]
            for t in below:
                tiles[t] = jnp.where(own, 0.0, tiles[t]) - total([below[t][k] * right[k] for k in range(STEP)])
            far = after + wide
            if far < count:
                packed = [jnp.zeros_like(tiles[0])] * count
                for e in range(wide):
                    packed[step + e] = right[TILE * e]
                    for i in range(1, TILE):
                        packed[step + e] = jnp.where(rows == i, right[TILE * e + i], packed[step + e])
                product = dot_nn(jnp.concatenate(tiles[far:], axis=0), jnp.concatenate(packed, axis=0))
                for t in range(far, count):
                    tiles[t] = jnp.where(own, 0.0, tiles[t]) - product[TILE * (t - far) : TILE * (t - far + 1)]
        for e in range(wide):
            diagonal, within = jnp.ones_like(forward[e]), jnp.zeros_like(forward[e])
            for i in range(0, TILE, 2):
                a, b, _, det, _ = pivots[(TILE * e + i) // 2]
                inverse = pl.reciprocal(a, approx=False)
                diagonal = jnp.where(rows == i, a, jnp.where(rows == i + 1, det * inverse, diagonal))
                within = jnp.where(rows == i + 1, b * inverse * sublane(forward[e], i), within)
            out.append((forward[e] - within) * lax.rsqrt(diagonal))
    return out


def assemble(my_row, core, found, mirrored, work):
    for (i, j), carrier in CARRIED:
        for d in range(len(found)):

            @pl.when((my_row ^ i) == d)
            def _():
                block = jnp.where(core == carrier, found[d][...], mirrored[d][...])
                if j > i:
                    work[j * NB : (j + 1) * NB, i * NB : (i + 1) * NB] = block.T
                else:
                    work[i * NB : (i + 1) * NB, j * NB : (j + 1) * NB] = block


def head_kernel(begin, end, place_ref, *refs):
    inverse_ref, work = refs[-2:]
    if begin == 0:
        count = (len(refs) - 2) // 2
        assemble(place_ref[0], place_ref[1] % 2, refs[:count], refs[count : 2 * count], work)
    else:
        inverse_ref[0, :HALF, :HALF] = refs[0][...]
        work[...] = refs[1][...]
    low = lax.broadcasted_iota(jnp.int32, (HALF, HALF), 0) >= lax.broadcasted_iota(jnp.int32, (HALF, HALF), 1)
    for at in range(begin, end):
        left, right = at * HALF, (at + 1) * HALF
        block = work[left:right, left:right]
        tiles = [block[TILE * i : TILE * (i + 1)] for i in range(HALF // TILE)]
        inverse = jnp.where(low, jnp.concatenate(invert_factor(tiles), axis=0), 0.0)
        if begin == 0:
            inverse_ref[...] = inverse
        else:
            diagonal = slice((at % 2) * HALF, (at % 2 + 1) * HALF)
            inverse_ref[at // 2, diagonal, diagonal] = inverse
        work[left:right, left:right] = jnp.where(low, dot_nt(block, inverse), 0.0)
        if right < HEAD:
            solved = dot_nt(work[right:, left:right], inverse)
            work[right:, left:right] = solved
            for column in range(right, HEAD, HALF):
                part = solved[column - right :]
                part = work[column:, column : column + HALF] - dot_nt(part, part[:HALF])
                work[column:, column : column + HALF] = part
        if begin and at % 2:
            k = at // 2
            first, second = inverse_ref[k, :HALF, :HALF], inverse_ref[k, HALF:, HALF:]
            below = work[left:right, left - HALF : left]
            inverse_ref[k, HALF:, :HALF] = -dot_nn(second, dot_nn(below, first))
            inverse_ref[k, :HALF, HALF:] = jnp.zeros((HALF, HALF), jnp.float32)
            work[left - HALF : left, left:right] = jnp.zeros((HALF, HALF), jnp.float32)


def factor_head(begin, end, place, *blocks):
    return pl.pallas_call(
        functools.partial(head_kernel, begin, end),
        out_shape=[
            jax.ShapeDtypeStruct((PANELS, NB, NB) if begin else (HALF, HALF), jnp.float32),
            jax.ShapeDtypeStruct((HEAD, HEAD), jnp.float32),
        ],
        in_specs=[pl.BlockSpec(memory_space=pltpu.SMEM)] + [pl.BlockSpec(memory_space=pltpu.VMEM)] * len(blocks),
        out_specs=[pl.BlockSpec(memory_space=pltpu.VMEM)] * 2,
        cost_estimate=pl.CostEstimate(flops=1_000, bytes_accessed=1_000, transcendentals=0),
        compiler_params=pltpu.CompilerParams(vmem_limit_bytes=(14 if begin else 56) * MIB),
        name="factor_head",
    )(place, *blocks)


def across_kernel(place_ref, inverse_ref, head_ref, *refs):
    heads, across = refs[:-1], refs[-1]
    inverse, lower = head_blocks(inverse_ref, head_ref)
    for j in range(PANELS):
        raw = heads[0][...]
        for d in range(1, len(heads)):
            raw = jnp.where((place_ref[0] ^ j) == d, heads[d][...], raw)
        for i in range(j):
            raw = raw - dot_nn(lower[j, i][...], across[i * NB : (i + 1) * NB])
        across[j * NB : (j + 1) * NB] = dot_nn(inverse[j][...], raw)


def head_blocks(inverse_ref, head_ref):
    inverse = [inverse_ref.at[j] for j in range(PANELS)]
    lower = {
        (i, j): head_ref.at[i * NB : (i + 1) * NB, j * NB : (j + 1) * NB] for i, j in ((1, 0), (2, 0), (2, 1))
    }
    return inverse, lower


def solve_across(place, inverse, head, heads):
    whole = pl.BlockSpec(memory_space=pltpu.VMEM)
    return pl.pallas_call(
        across_kernel,
        out_shape=jax.ShapeDtypeStruct((HEAD, heads[0].shape[1]), jnp.float32),
        in_specs=[pl.BlockSpec(memory_space=pltpu.SMEM)] + [whole] * (2 + len(heads)),
        out_specs=whole,
        cost_estimate=pl.CostEstimate(flops=4_000_000_000, bytes_accessed=5_000_000, transcendentals=0),
        compiler_params=pltpu.CompilerParams(vmem_limit_bytes=(20 if len(heads) <= 4 else 56) * MIB),
        name="solve_across",
    )(place, inverse, head, *heads)


def update_kernel(grid_rows, place_ref, inverse_ref, head_ref, top_ref, top_other_ref, *refs):
    held_ref, held_other_ref, swapped_ref, swapped_other_ref, across, matrix_ref, out_ref, solved = refs
    my_row, my_col = place_ref[0], place_ref[1]
    plane, core = my_col // 2, my_col % 2
    step = pl.program_id(0)
    inverse, lower = head_blocks(inverse_ref, head_ref)

    @pl.when(step == 0)
    def _():
        def by_core(mine, other):
            return jnp.where(core == 0, mine, other)

        held, held_other = held_ref[...], held_other_ref[...]
        swapped, swapped_other = swapped_ref[...], swapped_other_ref[...]
        even = plane % 2 == 0
        own, across_core = jnp.where(even, held, swapped), jnp.where(even, held_other, swapped_other)
        last = jnp.where(even, by_core(swapped, swapped_other), by_core(held, held_other))
        first, second, third = top_ref[0], top_other_ref[0], by_core(top_ref[1], top_other_ref[1])
        raw = [
            jnp.concatenate([by_core(first, second), by_core(own, across_core)], axis=0),
            jnp.concatenate([by_core(second, first), by_core(across_core, own)], axis=0),
            jnp.concatenate([third, last], axis=0),
        ]
        depth = solved.shape[0] // 2
        for j in range(PANELS):
            there = slice(j * NB, (j + 1) * NB)
            for here in (slice(0, depth), slice(depth, 2 * depth)):
                rest = raw[j][here]
                for i in range(j):
                    rest = rest - dot_nt(solved[here, i * NB : (i + 1) * NB], lower[j, i][...])
                solved[here, there] = dot_nt(rest, inverse[j][...])

    depth = out_ref.shape[0]
    product = dot_nn(solved[pl.ds(pl.multiple_of(step * depth, depth), depth), :], across[...])
    head_row = pl.ds(pl.multiple_of(jnp.minimum(my_row, PANELS - 1) * NB, NB), NB)
    head_col = pl.ds(pl.multiple_of(jnp.minimum(my_col, PANELS - 1) * NB, NB), NB)
    for block in range(depth // NB):
        slot = step * (depth // NB) + block
        row = my_row + grid_rows * slot
        here = slice(block * NB, (block + 1) * NB)
        mine = solved[pl.ds(pl.multiple_of(slot * NB, NB), NB), :]
        for t in range(out_ref.shape[1] // NB):
            there = slice(t * NB, (t + 1) * NB)
            updated = matrix_ref[here, there] - product[here, there]
            updated = jnp.where(row < PANELS, 0.0, updated)
            if t == 0:
                panel = mine[:, :NB]
                for j in range(1, PANELS):
                    panel = jnp.where(my_col == j, mine[:, j * NB : (j + 1) * NB], panel)
                factor = jnp.where(my_col <= row, head_ref[head_row, head_col], 0.0)
                panel = jnp.where(row < PANELS, factor, panel)
                updated = jnp.where(my_col < PANELS, panel, updated)
            out_ref[here, there] = updated


def update(grid_rows, place, inverse, head, top, top_other, sent, across, matrix):
    whole = pl.BlockSpec(memory_space=pltpu.VMEM)
    depth = 2 * NB if matrix.shape[0] % (2 * NB) == 0 else NB
    strip = pl.BlockSpec((depth, matrix.shape[1]), lambda step: (step, 0))
    return pl.pallas_call(
        functools.partial(update_kernel, grid_rows),
        out_shape=jax.ShapeDtypeStruct(matrix.shape, jnp.float32),
        grid=(matrix.shape[0] // depth,),
        in_specs=[pl.BlockSpec(memory_space=pltpu.SMEM)] + [whole] * (5 + len(sent)) + [strip],
        out_specs=strip,
        scratch_shapes=[pltpu.VMEM((matrix.shape[0], HEAD), jnp.float32)],
        cost_estimate=pl.CostEstimate(flops=10_000_000_000, bytes_accessed=10_000_000, transcendentals=0),
        compiler_params=pltpu.CompilerParams(vmem_limit_bytes=30 * MIB),
        name="update",
    )(place, inverse, head, top, top_other, *sent, across, matrix)


def body(matrix):
    grid_rows, grid_cols = lax.axis_size("row"), lax.axis_size("col")
    planes = grid_cols // 2
    my_row, my_col = lax.axis_index("row"), lax.axis_index("col")
    plane, core = my_col // 2, my_col % 2

    def send(x, pairs):
        flat = [(a * grid_cols + b, c * grid_cols + d) for (a, b), (c, d) in pairs]
        return lax.ppermute(x, ("row", "col"), flat)

    def swap_cores(x):
        return send(x, [((r, c), (r, c ^ 1)) for r in range(grid_rows) for c in range(grid_cols)])

    def along_rows(x, begin, end):
        out = []
        for d in range(begin, end):
            pairs = [((i, c), (i ^ d, c)) for i in range(PANELS) if i ^ d < grid_rows for c in range(grid_cols)]
            out.append(send(x, pairs) if d else x)
        return out

    place = jnp.stack([my_row, my_col]).astype(jnp.int32)
    corner, matrix = lax.optimization_barrier((matrix[:NB, :NB], matrix))
    carried = jnp.zeros_like(corner)
    passed = []
    for d in [*range(1, planes), 0]:
        pairs = []
        for (i, j), carrier in CARRIED:
            target = 2 * ((j // 2 + d) % planes) + carrier
            if target != j:
                pairs.append(((i, j), (i, target)))
        if d:
            for r in range(PANELS, grid_rows):
                pairs += [((r, q), (r, 2 * d + q)) for q in range(2)]
                pairs.append(((r, 2), (r, 2 * ((1 + d) % planes))))
        passed.append(send(corner, pairs))
        carried = carried + passed[-1]
    native = jnp.zeros((), jnp.bool_)
    for (i, j), carrier in CARRIED:
        if j % 2 == carrier:
            native = native | ((my_row == i) & (my_col == j))
    carried = jnp.where(native, corner, carried)
    heads = along_rows(matrix[:NB], 0, EARLY)
    carried, heads, place = lax.optimization_barrier((carried, heads, place))
    found = along_rows(carried, 0, grid_rows)
    top_mine, top_last = corner, corner
    for d in range(1, planes):
        top_mine = jnp.where(plane == d, passed[d - 1], top_mine)
        top_last = jnp.where((plane - 1) % planes == d, passed[d - 1], top_last)
    found, top = lax.optimization_barrier((found, jnp.stack([top_mine, top_last])))
    mirrored = [swap_cores(x) for x in found]
    strip, _ = lax.optimization_barrier((matrix[NB:, :NB], carried))

    held = strip
    distance = planes // 2
    while distance > 1:
        pairs = []
        for z in range(0, planes, 2 * distance):
            for r in range(grid_rows):
                pairs += [((r, 2 * z + q), (r, 2 * (z + distance) + q)) for q in range(2)]
                pairs.append(((r, 2 * z + 2), (r, 2 * (z + distance) + 2)))
        got = send(held, pairs)
        if distance == 2:
            early, head = factor_head(0, 1, place, *found, *mirrored)
            got, head, late_matrix = lax.optimization_barrier((got, head, matrix))
            heads += along_rows(late_matrix[:NB], EARLY, grid_rows)
        held = jnp.where((plane // distance) % 2 == 1, got, held)
        distance //= 2
    held, head, top = lax.optimization_barrier((held, head, top))
    pairs = []
    for z in range(0, planes, 2):
        for r in range(grid_rows):
            pairs += [((r, 2 * z + q), (r, 2 * z + 2 + q)) for q in range(2)]
            pairs.append(((r, 2 * z + 2), (r, 2 * z)))
    swapped = send(held, pairs)
    held_other, top_other = swap_cores(held), swap_cores(top)
    inverse, head = factor_head(1, HEAD // HALF, place, early, head)
    across = solve_across(place, inverse, head, heads)
    swapped, across = lax.optimization_barrier((swapped, across))
    swapped_other = swap_cores(swapped)
    sent = [held, held_other, swapped, swapped_other]
    return update(grid_rows, place, inverse, head, top, top_other, sent, across, matrix)


def solution(mesh):
    return jax.shard_map(body, mesh=mesh, in_specs=(P("row", "col"),), out_specs=P("row", "col"), check_vma=False)
```

```python
import functools

import jax
import jax.numpy as jnp
from jax import lax
from jax.experimental import pallas as pl
from jax.experimental.pallas import tpu as pltpu
from jax.sharding import PartitionSpec as P

NB = 256
PANELS = 3
HALF = 128
TILE = 8
STEP = 16
EARLY = 3
HEAD = PANELS * NB
MIB = 1024 * 1024

CARRIED = (((0, 0), 0), ((0, 1), 1), ((1, 2), 0), ((1, 1), 1), ((2, 0), 0), ((2, 2), 1))


def sublane(x, k):
    return jnp.broadcast_to(x[k : k + 1, :], x.shape)


def lane(x, k):
    return jnp.broadcast_to(x[:, k : k + 1], x.shape)


def dot_nt(a, b):
    return lax.dot_general(
        a, b, (((1,), (1,)), ((), ())), precision=lax.Precision.HIGHEST, preferred_element_type=jnp.float32
    )


def dot_nn(a, b):
    return jnp.dot(a, b, precision=lax.Precision.HIGHEST, preferred_element_type=jnp.float32)


def opaque(x):
    return jnp.maximum(x, -3.0e38)


def total(terms):
    while len(terms) > 1:
        terms = [sum(terms[i : i + 2][1:], terms[i]) for i in range(0, len(terms), 2)]
    return terms[0]


def invert_factor(tiles):
    count, wide = len(tiles), STEP // TILE
    rows = lax.broadcasted_iota(jnp.int32, (TILE, HALF), 0)
    lanes = lax.broadcasted_iota(jnp.int32, (TILE, HALF), 1)
    out = []
    for step in range(0, count, wide):
        start, after = TILE * step, step + wide
        own = (lanes >= start) & (lanes < start + STEP)
        column = [[opaque(lane(tiles[step + e], start + k)) for e in range(wide)] for k in range(STEP)]
        forward = [
            jnp.where(own, jnp.where(lanes - start == rows + TILE * e, 1.0, 0.0), tiles[step + e]) for e in range(wide)
        ]
        solved, pivots, below = list(forward), [], {}
        for k in range(0, STEP, 2):
            o, i = k // TILE, k % TILE
            a, b, c = sublane(column[k][o], i), sublane(column[k + 1][o], i), sublane(column[k + 1][o], i + 1)
            det = a * c - b * b
            inverse = pl.reciprocal(det, approx=False)
            pivots.append((a, b, c, det, inverse))
            if k == 0:
                zero = jnp.minimum(jnp.abs(inverse), 0.0)
                for t in range(after, min(after + wide, count)):
                    below[t] = [lane(tiles[t] + zero, start + j) for j in range(STEP)]
            one = [column[k][e] * c - column[k + 1][e] * b for e in range(wide)]
            two = [column[k + 1][e] * a - column[k][e] * b for e in range(wide)]
            pair = (rows == i) | (rows == i + 1)
            one[o], two[o] = jnp.where(pair, 0.0, one[o]), jnp.where(pair, 0.0, two[o])
            first, second = [x * inverse for x in one], [x * inverse for x in two]
            for j in range(k + 2, STEP):
                u, v = sublane(column[j][o], i), sublane(column[j][o], i + 1)
                for e in range(wide):
                    if j < k + 4:
                        column[j][e] = column[j][e] - (one[e] * u + two[e] * v) * inverse
                    else:
                        column[j][e] = column[j][e] - (first[e] * u + second[e] * v)
            u, v = sublane(forward[o], i), sublane(forward[o], i + 1)
            x, y = sublane(solved[o], i), sublane(solved[o], i + 1)
            for e in range(wide):
                if after < count:
                    solved[e] = solved[e] - (first[e] * x + second[e] * y)
                if e > o:
                    forward[e] = forward[e] - (first[e] * u + second[e] * v)
                elif e == o and i + 2 < TILE:
                    forward[e] = forward[e] - jnp.where(rows > i, first[e] * u + second[e] * v, 0.0)
        if after < count:
            right = []
            for k in range(0, STEP, 2):
                o, i = k // TILE, k % TILE
                a, b, c, _, inverse = pivots[k // 2]
                x, y = sublane(solved[o], i), sublane(solved[o], i + 1)
                right += [(x * c - y * b) * inverse, (y * a - x * b) * inverse]
            for t in below:
                tiles[t] = jnp.where(own, 0.0, tiles[t]) - total([below[t][k] * right[k] for k in range(STEP)])
            far = after + wide
            if far < count:
                packed = [jnp.zeros_like(tiles[0])] * count
                for e in range(wide):
                    packed[step + e] = right[TILE * e]
                    for i in range(1, TILE):
                        packed[step + e] = jnp.where(rows == i, right[TILE * e + i], packed[step + e])
                product = dot_nn(jnp.concatenate(tiles[far:], axis=0), jnp.concatenate(packed, axis=0))
                for t in range(far, count):
                    tiles[t] = jnp.where(own, 0.0, tiles[t]) - product[TILE * (t - far) : TILE * (t - far + 1)]
        for e in range(wide):
            diagonal, within = jnp.ones_like(forward[e]), jnp.zeros_like(forward[e])
            for i in range(0, TILE, 2):
                a, b, _, det, _ = pivots[(TILE * e + i) // 2]
                inverse = pl.reciprocal(a, approx=False)
                diagonal = jnp.where(rows == i, a, jnp.where(rows == i + 1, det * inverse, diagonal))
                within = jnp.where(rows == i + 1, b * inverse * sublane(forward[e], i), within)
            out.append((forward[e] - within) * lax.rsqrt(diagonal))
    return out


def assemble(my_row, core, found, mirrored, work):
    for (i, j), carrier in CARRIED:
        for d in range(len(found)):

            @pl.when((my_row ^ i) == d)
            def _():
                block = jnp.where(core == carrier, found[d][...], mirrored[d][...])
                if j > i:
                    work[j * NB : (j + 1) * NB, i * NB : (i + 1) * NB] = block.T
                else:
                    work[i * NB : (i + 1) * NB, j * NB : (j + 1) * NB] = block


def head_kernel(begin, end, place_ref, *refs):
    inverse_ref, work = refs[-2:]
    if begin == 0:
        count = (len(refs) - 2) // 2
        assemble(place_ref[0], place_ref[1] % 2, refs[:count], refs[count : 2 * count], work)
    else:
        inverse_ref[0, :HALF, :HALF] = refs[0][...]
        work[...] = refs[1][...]
    low = lax.broadcasted_iota(jnp.int32, (HALF, HALF), 0) >= lax.broadcasted_iota(jnp.int32, (HALF, HALF), 1)
    for at in range(begin, end):
        left, right = at * HALF, (at + 1) * HALF
        block = work[left:right, left:right]
        tiles = [block[TILE * i : TILE * (i + 1)] for i in range(HALF // TILE)]
        inverse = jnp.where(low, jnp.concatenate(invert_factor(tiles), axis=0), 0.0)
        if begin == 0:
            inverse_ref[...] = inverse
        else:
            diagonal = slice((at % 2) * HALF, (at % 2 + 1) * HALF)
            inverse_ref[at // 2, diagonal, diagonal] = inverse
        work[left:right, left:right] = jnp.where(low, dot_nt(block, inverse), 0.0)
        if right < HEAD:
            solved = dot_nt(work[right:, left:right], inverse)
            work[right:, left:right] = solved
            for column in range(right, HEAD, HALF):
                part = solved[column - right :]
                part = work[column:, column : column + HALF] - dot_nt(part, part[:HALF])
                work[column:, column : column + HALF] = part
        if begin and at % 2:
            k = at // 2
            first, second = inverse_ref[k, :HALF, :HALF], inverse_ref[k, HALF:, HALF:]
            below = work[left:right, left - HALF : left]
            inverse_ref[k, HALF:, :HALF] = -dot_nn(second, dot_nn(below, first))
            inverse_ref[k, :HALF, HALF:] = jnp.zeros((HALF, HALF), jnp.float32)
            work[left - HALF : left, left:right] = jnp.zeros((HALF, HALF), jnp.float32)


def factor_head(begin, end, place, *blocks):
    return pl.pallas_call(
        functools.partial(head_kernel, begin, end),
        out_shape=[
            jax.ShapeDtypeStruct((PANELS, NB, NB) if begin else (HALF, HALF), jnp.float32),
            jax.ShapeDtypeStruct((HEAD, HEAD), jnp.float32),
        ],
        in_specs=[pl.BlockSpec(memory_space=pltpu.SMEM)] + [pl.BlockSpec(memory_space=pltpu.VMEM)] * len(blocks),
        out_specs=[pl.BlockSpec(memory_space=pltpu.VMEM)] * 2,
        cost_estimate=pl.CostEstimate(flops=15_000_000_000 if begin else 1_000, bytes_accessed=1_000, transcendentals=0),
        compiler_params=pltpu.CompilerParams(vmem_limit_bytes=(14 if begin else 56) * MIB),
        name="factor_head",
    )(place, *blocks)


def across_kernel(begin, end, place_ref, inverse_ref, head_ref, *refs):
    heads, across = refs[: len(refs) - 1 - (begin > 0)], refs[-1]
    inverse, lower = head_blocks(inverse_ref, head_ref)
    if begin:
        across[: begin * NB] = refs[-2][...]
    for j in range(begin, end):
        raw = heads[0][...]
        for d in range(1, len(heads)):
            raw = jnp.where((place_ref[0] ^ j) == d, heads[d][...], raw)
        for i in range(j):
            raw = raw - dot_nn(lower[j, i][...], across[i * NB : (i + 1) * NB])
        across[j * NB : (j + 1) * NB] = dot_nn(inverse[j][...], raw)


def head_blocks(inverse_ref, head_ref):
    inverse = [inverse_ref.at[j] for j in range(PANELS)]
    lower = {
        (i, j): head_ref.at[i * NB : (i + 1) * NB, j * NB : (j + 1) * NB] for i, j in ((1, 0), (2, 0), (2, 1))
    }
    return inverse, lower


def solve_across(begin, end, place, inverse, head, heads, *given):
    whole = pl.BlockSpec(memory_space=pltpu.VMEM)
    return pl.pallas_call(
        functools.partial(across_kernel, begin, end),
        out_shape=jax.ShapeDtypeStruct((end * NB, heads[0].shape[1]), jnp.float32),
        in_specs=[pl.BlockSpec(memory_space=pltpu.SMEM)] + [whole] * (2 + len(heads) + len(given)),
        out_specs=whole,
        cost_estimate=pl.CostEstimate(flops=4_000_000_000, bytes_accessed=5_000_000, transcendentals=0),
        compiler_params=pltpu.CompilerParams(vmem_limit_bytes=(20 if len(heads) <= 4 else 56) * MIB),
        name="solve_across",
    )(place, inverse, head, *heads, *given)


def update_kernel(grid_rows, place_ref, inverse_ref, head_ref, top_ref, top_other_ref, *refs):
    held_ref, held_other_ref, swapped_ref, swapped_other_ref, across, matrix_ref, out_ref, solved = refs
    my_row, my_col = place_ref[0], place_ref[1]
    plane, core = my_col // 2, my_col % 2
    step = pl.program_id(0)
    inverse, lower = head_blocks(inverse_ref, head_ref)

    @pl.when(step == 0)
    def _():
        def by_core(mine, other):
            return jnp.where(core == 0, mine, other)

        held, held_other = held_ref[...], held_other_ref[...]
        swapped, swapped_other = swapped_ref[...], swapped_other_ref[...]
        even = plane % 2 == 0
        own, across_core = jnp.where(even, held, swapped), jnp.where(even, held_other, swapped_other)
        last = jnp.where(even, by_core(swapped, swapped_other), by_core(held, held_other))
        first, second, third = top_ref[0], top_other_ref[0], by_core(top_ref[1], top_other_ref[1])
        raw = [
            jnp.concatenate([by_core(first, second), by_core(own, across_core)], axis=0),
            jnp.concatenate([by_core(second, first), by_core(across_core, own)], axis=0),
            jnp.concatenate([third, last], axis=0),
        ]
        depth = solved.shape[0] // 2
        for j in range(PANELS):
            there = slice(j * NB, (j + 1) * NB)
            for here in (slice(0, depth), slice(depth, 2 * depth)):
                rest = raw[j][here]
                for i in range(j):
                    rest = rest - dot_nt(solved[here, i * NB : (i + 1) * NB], lower[j, i][...])
                solved[here, there] = dot_nt(rest, inverse[j][...])

    depth = out_ref.shape[0]
    product = dot_nn(solved[pl.ds(pl.multiple_of(step * depth, depth), depth), :], across[...])
    head_row = pl.ds(pl.multiple_of(jnp.minimum(my_row, PANELS - 1) * NB, NB), NB)
    head_col = pl.ds(pl.multiple_of(jnp.minimum(my_col, PANELS - 1) * NB, NB), NB)
    for block in range(depth // NB):
        slot = step * (depth // NB) + block
        row = my_row + grid_rows * slot
        here = slice(block * NB, (block + 1) * NB)
        mine = solved[pl.ds(pl.multiple_of(slot * NB, NB), NB), :]
        for t in range(out_ref.shape[1] // NB):
            there = slice(t * NB, (t + 1) * NB)
            updated = matrix_ref[here, there] - product[here, there]
            updated = jnp.where(row < PANELS, 0.0, updated)
            if t == 0:
                panel = mine[:, :NB]
                for j in range(1, PANELS):
                    panel = jnp.where(my_col == j, mine[:, j * NB : (j + 1) * NB], panel)
                factor = jnp.where(my_col <= row, head_ref[head_row, head_col], 0.0)
                panel = jnp.where(row < PANELS, factor, panel)
                updated = jnp.where(my_col < PANELS, panel, updated)
            out_ref[here, there] = updated


def update(grid_rows, place, inverse, head, top, top_other, sent, across, matrix):
    whole = pl.BlockSpec(memory_space=pltpu.VMEM)
    depth = 2 * NB if matrix.shape[0] % (2 * NB) == 0 else NB
    strip = pl.BlockSpec((depth, matrix.shape[1]), lambda step: (step, 0))
    return pl.pallas_call(
        functools.partial(update_kernel, grid_rows),
        out_shape=jax.ShapeDtypeStruct(matrix.shape, jnp.float32),
        grid=(matrix.shape[0] // depth,),
        in_specs=[pl.BlockSpec(memory_space=pltpu.SMEM)] + [whole] * (5 + len(sent)) + [strip],
        out_specs=strip,
        scratch_shapes=[pltpu.VMEM((matrix.shape[0], HEAD), jnp.float32)],
        cost_estimate=pl.CostEstimate(flops=10_000_000_000, bytes_accessed=10_000_000, transcendentals=0),
        compiler_params=pltpu.CompilerParams(vmem_limit_bytes=30 * MIB),
        name="update",
    )(place, inverse, head, top, top_other, *sent, across, matrix)


def body(matrix):
    grid_rows, grid_cols = lax.axis_size("row"), lax.axis_size("col")
    planes = grid_cols // 2
    my_row, my_col = lax.axis_index("row"), lax.axis_index("col")
    plane, core = my_col // 2, my_col % 2

    def send(x, pairs):
        flat = [(a * grid_cols + b, c * grid_cols + d) for (a, b), (c, d) in pairs]
        return lax.ppermute(x, ("row", "col"), flat)

    def swap_cores(x):
        return send(x, [((r, c), (r, c ^ 1)) for r in range(grid_rows) for c in range(grid_cols)])

    def along_rows(x, begin, end):
        out = []
        for d in range(begin, end):
            pairs = [((i, c), (i ^ d, c)) for i in range(PANELS) if i ^ d < grid_rows for c in range(grid_cols)]
            out.append(send(x, pairs) if d else x)
        return out

    place = jnp.stack([my_row, my_col]).astype(jnp.int32)
    corner, matrix = lax.optimization_barrier((matrix[:NB, :NB], matrix))
    carried = jnp.zeros_like(corner)
    passed = []
    for d in [*range(1, planes), 0]:
        pairs = []
        for (i, j), carrier in CARRIED:
            target = 2 * ((j // 2 + d) % planes) + carrier
            if target != j:
                pairs.append(((i, j), (i, target)))
        if d:
            for r in range(PANELS, grid_rows):
                pairs += [((r, q), (r, 2 * d + q)) for q in range(2)]
                pairs.append(((r, 2), (r, 2 * ((1 + d) % planes))))
        passed.append(send(corner, pairs))
        carried = carried + passed[-1]
    native = jnp.zeros((), jnp.bool_)
    for (i, j), carrier in CARRIED:
        if j % 2 == carrier:
            native = native | ((my_row == i) & (my_col == j))
    carried = jnp.where(native, corner, carried)
    heads = along_rows(matrix[:NB], 0, EARLY)
    carried, heads, place = lax.optimization_barrier((carried, heads, place))
    found = along_rows(carried, 0, grid_rows)
    top_mine, top_last = corner, corner
    for d in range(1, planes):
        top_mine = jnp.where(plane == d, passed[d - 1], top_mine)
        top_last = jnp.where((plane - 1) % planes == d, passed[d - 1], top_last)
    found, top = lax.optimization_barrier((found, jnp.stack([top_mine, top_last])))
    mirrored = [swap_cores(x) for x in found]
    strip, _ = lax.optimization_barrier((matrix[NB:, :NB], carried))

    held = strip
    distance = planes // 2
    while distance > 1:
        pairs = []
        for z in range(0, planes, 2 * distance):
            for r in range(grid_rows):
                pairs += [((r, 2 * z + q), (r, 2 * (z + distance) + q)) for q in range(2)]
                pairs.append(((r, 2 * z + 2), (r, 2 * (z + distance) + 2)))
        got = send(held, pairs)
        if distance == 2:
            early, head = factor_head(0, 1, place, *found, *mirrored)
            got, head, late_matrix = lax.optimization_barrier((got, head, matrix))
            heads += along_rows(late_matrix[:NB], EARLY, grid_rows)
        held = jnp.where((plane // distance) % 2 == 1, got, held)
        distance //= 2
    held, head, top = lax.optimization_barrier((held, head, top))
    pairs = []
    for z in range(0, planes, 2):
        for r in range(grid_rows):
            pairs += [((r, 2 * z + q), (r, 2 * z + 2 + q)) for q in range(2)]
            pairs.append(((r, 2 * z + 2), (r, 2 * z)))
    swapped = send(held, pairs)
    held_other, top_other = swap_cores(held), swap_cores(top)
    inverse, head = factor_head(1, HEAD // HALF, place, early, head)
    across = solve_across(0, 1, place, inverse, head, heads)
    swapped, across = lax.optimization_barrier((swapped, across))
    swapped_other = swap_cores(swapped)
    across = solve_across(1, PANELS, place, inverse, head, heads, across)
    sent = [held, held_other, swapped, swapped_other]
    return update(grid_rows, place, inverse, head, top, top_other, sent, across, matrix)


def solution(mesh):
    return jax.shard_map(body, mesh=mesh, in_specs=(P("row", "col"),), out_specs=P("row", "col"), check_vma=False)
```

```python
import functools

import jax
import jax.numpy as jnp
from jax import lax
from jax.experimental import pallas as pl
from jax.experimental.pallas import tpu as pltpu
from jax.sharding import PartitionSpec as P

NB = 256
PANELS = 3
HALF = 128
TILE = 8
STEP = 16
EARLY = 3
HEAD = PANELS * NB
MIB = 1024 * 1024

CARRIED = (((0, 0), 0), ((0, 1), 1), ((1, 2), 0), ((1, 1), 1), ((2, 0), 0), ((2, 2), 1))


def sublane(x, k):
    return jnp.broadcast_to(x[k : k + 1, :], x.shape)


def lane(x, k):
    return jnp.broadcast_to(x[:, k : k + 1], x.shape)


def dot_nt(a, b):
    return lax.dot_general(
        a, b, (((1,), (1,)), ((), ())), precision=lax.Precision.HIGHEST, preferred_element_type=jnp.float32
    )


def dot_nn(a, b):
    return jnp.dot(a, b, precision=lax.Precision.HIGHEST, preferred_element_type=jnp.float32)


def opaque(x):
    return jnp.maximum(x, -3.0e38)


def total(terms):
    while len(terms) > 1:
        terms = [sum(terms[i : i + 2][1:], terms[i]) for i in range(0, len(terms), 2)]
    return terms[0]


def invert_factor(tiles):
    count, wide = len(tiles), STEP // TILE
    rows = lax.broadcasted_iota(jnp.int32, (TILE, HALF), 0)
    lanes = lax.broadcasted_iota(jnp.int32, (TILE, HALF), 1)
    out = []
    for step in range(0, count, wide):
        start, after = TILE * step, step + wide
        own = (lanes >= start) & (lanes < start + STEP)
        column = [[opaque(lane(tiles[step + e], start + k)) for e in range(wide)] for k in range(STEP)]
        forward = [
            jnp.where(own, jnp.where(lanes - start == rows + TILE * e, 1.0, 0.0), tiles[step + e]) for e in range(wide)
        ]
        solved, pivots, below = list(forward), [], {}
        for k in range(0, STEP, 2):
            o, i = k // TILE, k % TILE
            a, b, c = sublane(column[k][o], i), sublane(column[k + 1][o], i), sublane(column[k + 1][o], i + 1)
            det = a * c - b * b
            inverse = pl.reciprocal(det, approx=False)
            pivots.append((a, b, c, det, inverse))
            if k == 0:
                zero = jnp.minimum(jnp.abs(inverse), 0.0)
                for t in range(after, min(after + wide, count)):
                    below[t] = [lane(tiles[t] + zero, start + j) for j in range(STEP)]
            one = [column[k][e] * c - column[k + 1][e] * b for e in range(wide)]
            two = [column[k + 1][e] * a - column[k][e] * b for e in range(wide)]
            pair = (rows == i) | (rows == i + 1)
            one[o], two[o] = jnp.where(pair, 0.0, one[o]), jnp.where(pair, 0.0, two[o])
            first, second = [x * inverse for x in one], [x * inverse for x in two]
            for j in range(k + 2, STEP):
                u, v = sublane(column[j][o], i), sublane(column[j][o], i + 1)
                for e in range(wide):
                    if j < k + 4:
                        column[j][e] = column[j][e] - (one[e] * u + two[e] * v) * inverse
                    else:
                        column[j][e] = column[j][e] - (first[e] * u + second[e] * v)
            u, v = sublane(forward[o], i), sublane(forward[o], i + 1)
            x, y = sublane(solved[o], i), sublane(solved[o], i + 1)
            for e in range(wide):
                if after < count:
                    solved[e] = solved[e] - (first[e] * x + second[e] * y)
                if e > o:
                    forward[e] = forward[e] - (first[e] * u + second[e] * v)
                elif e == o and i + 2 < TILE:
                    forward[e] = forward[e] - jnp.where(rows > i, first[e] * u + second[e] * v, 0.0)
        if after < count:
            right = []
            for k in range(0, STEP, 2):
                o, i = k // TILE, k % TILE
                a, b, c, _, inverse = pivots[k // 2]
                x, y = sublane(solved[o], i), sublane(solved[o], i + 1)
                right += [(x * c - y * b) * inverse, (y * a - x * b) * inverse]
            for t in below:
                tiles[t] = jnp.where(own, 0.0, tiles[t]) - total([below[t][k] * right[k] for k in range(STEP)])
            far = after + wide
            if far < count:
                packed = [jnp.zeros_like(tiles[0])] * count
                for e in range(wide):
                    packed[step + e] = right[TILE * e]
                    for i in range(1, TILE):
                        packed[step + e] = jnp.where(rows == i, right[TILE * e + i], packed[step + e])
                product = dot_nn(jnp.concatenate(tiles[far:], axis=0), jnp.concatenate(packed, axis=0))
                for t in range(far, count):
                    tiles[t] = jnp.where(own, 0.0, tiles[t]) - product[TILE * (t - far) : TILE * (t - far + 1)]
        for e in range(wide):
            diagonal, within = jnp.ones_like(forward[e]), jnp.zeros_like(forward[e])
            for i in range(0, TILE, 2):
                a, b, _, det, _ = pivots[(TILE * e + i) // 2]
                inverse = pl.reciprocal(a, approx=False)
                diagonal = jnp.where(rows == i, a, jnp.where(rows == i + 1, det * inverse, diagonal))
                within = jnp.where(rows == i + 1, b * inverse * sublane(forward[e], i), within)
            out.append((forward[e] - within) * lax.rsqrt(diagonal))
    return out


def assemble(my_row, core, found, mirrored, work):
    for (i, j), carrier in CARRIED:
        for d in range(len(found)):

            @pl.when((my_row ^ i) == d)
            def _():
                block = jnp.where(core == carrier, found[d][...], mirrored[d][...])
                if j > i:
                    work[j * NB : (j + 1) * NB, i * NB : (i + 1) * NB] = block.T
                else:
                    work[i * NB : (i + 1) * NB, j * NB : (j + 1) * NB] = block


def head_kernel(begin, end, place_ref, *refs):
    inverse_ref, work = refs[-2:]
    if begin == 0:
        count = (len(refs) - 2) // 2
        assemble(place_ref[0], place_ref[1] % 2, refs[:count], refs[count : 2 * count], work)
    else:
        inverse_ref[0, :HALF, :HALF] = refs[0][...]
        work[...] = refs[1][...]
    low = lax.broadcasted_iota(jnp.int32, (HALF, HALF), 0) >= lax.broadcasted_iota(jnp.int32, (HALF, HALF), 1)
    for at in range(begin, end):
        left, right = at * HALF, (at + 1) * HALF
        block = work[left:right, left:right]
        tiles = [block[TILE * i : TILE * (i + 1)] for i in range(HALF // TILE)]
        inverse = jnp.where(low, jnp.concatenate(invert_factor(tiles), axis=0), 0.0)
        if begin == 0:
            inverse_ref[...] = inverse
        else:
            diagonal = slice((at % 2) * HALF, (at % 2 + 1) * HALF)
            inverse_ref[at // 2, diagonal, diagonal] = inverse
        work[left:right, left:right] = jnp.where(low, dot_nt(block, inverse), 0.0)
        if right < HEAD:
            solved = dot_nt(work[right:, left:right], inverse)
            work[right:, left:right] = solved
            for column in range(right, HEAD, HALF):
                part = solved[column - right :]
                part = work[column:, column : column + HALF] - dot_nt(part, part[:HALF])
                work[column:, column : column + HALF] = part
        if begin and at % 2:
            k = at // 2
            first, second = inverse_ref[k, :HALF, :HALF], inverse_ref[k, HALF:, HALF:]
            below = work[left:right, left - HALF : left]
            inverse_ref[k, HALF:, :HALF] = -dot_nn(second, dot_nn(below, first))
            inverse_ref[k, :HALF, HALF:] = jnp.zeros((HALF, HALF), jnp.float32)
            work[left - HALF : left, left:right] = jnp.zeros((HALF, HALF), jnp.float32)


def factor_head(begin, end, place, *blocks):
    return pl.pallas_call(
        functools.partial(head_kernel, begin, end),
        out_shape=[
            jax.ShapeDtypeStruct((PANELS, NB, NB) if begin else (HALF, HALF), jnp.float32),
            jax.ShapeDtypeStruct((HEAD, HEAD), jnp.float32),
        ],
        in_specs=[pl.BlockSpec(memory_space=pltpu.SMEM)] + [pl.BlockSpec(memory_space=pltpu.VMEM)] * len(blocks),
        out_specs=[pl.BlockSpec(memory_space=pltpu.VMEM)] * 2,
        cost_estimate=pl.CostEstimate(flops=15_000_000_000 if begin else 1_000, bytes_accessed=1_000, transcendentals=0),
        compiler_params=pltpu.CompilerParams(vmem_limit_bytes=(14 if begin else 48) * MIB),
        name="factor_head",
    )(place, *blocks)


def across_kernel(begin, end, place_ref, inverse_ref, head_ref, *refs):
    heads, across = refs[: len(refs) - 1 - (begin > 0)], refs[-1]
    inverse, lower = head_blocks(inverse_ref, head_ref)
    if begin:
        across[: begin * NB] = refs[-2][...]
    for j in range(begin, end):
        raw = heads[0][...]
        for d in range(1, len(heads)):
            raw = jnp.where((place_ref[0] ^ j) == d, heads[d][...], raw)
        for i in range(j):
            raw = raw - dot_nn(lower[j, i][...], across[i * NB : (i + 1) * NB])
        across[j * NB : (j + 1) * NB] = dot_nn(inverse[j][...], raw)


def head_blocks(inverse_ref, head_ref):
    inverse = [inverse_ref.at[j] for j in range(PANELS)]
    lower = {
        (i, j): head_ref.at[i * NB : (i + 1) * NB, j * NB : (j + 1) * NB] for i, j in ((1, 0), (2, 0), (2, 1))
    }
    return inverse, lower


def solve_across(begin, end, place, inverse, head, heads, *given):
    whole = pl.BlockSpec(memory_space=pltpu.VMEM)
    return pl.pallas_call(
        functools.partial(across_kernel, begin, end),
        out_shape=jax.ShapeDtypeStruct((end * NB, heads[0].shape[1]), jnp.float32),
        in_specs=[pl.BlockSpec(memory_space=pltpu.SMEM)] + [whole] * (2 + len(heads) + len(given)),
        out_specs=whole,
        cost_estimate=pl.CostEstimate(flops=4_000_000_000, bytes_accessed=5_000_000, transcendentals=0),
        compiler_params=pltpu.CompilerParams(vmem_limit_bytes=(20 if len(heads) <= 4 else 56) * MIB),
        name="solve_across",
    )(place, inverse, head, *heads, *given)


def update_kernel(grid_rows, place_ref, inverse_ref, head_ref, top_ref, top_other_ref, *refs):
    held_ref, held_other_ref, swapped_ref, swapped_other_ref, across, matrix_ref, out_ref, solved = refs
    my_row, my_col = place_ref[0], place_ref[1]
    plane, core = my_col // 2, my_col % 2
    step = pl.program_id(0)
    inverse, lower = head_blocks(inverse_ref, head_ref)

    @pl.when(step == 0)
    def _():
        def by_core(mine, other):
            return jnp.where(core == 0, mine, other)

        held, held_other = held_ref[...], held_other_ref[...]
        swapped, swapped_other = swapped_ref[...], swapped_other_ref[...]
        even = plane % 2 == 0
        own, across_core = jnp.where(even, held, swapped), jnp.where(even, held_other, swapped_other)
        last = jnp.where(even, by_core(swapped, swapped_other), by_core(held, held_other))
        first, second, third = top_ref[0], top_other_ref[0], by_core(top_ref[1], top_other_ref[1])
        raw = [
            jnp.concatenate([by_core(first, second), by_core(own, across_core)], axis=0),
            jnp.concatenate([by_core(second, first), by_core(across_core, own)], axis=0),
            jnp.concatenate([third, last], axis=0),
        ]
        depth = solved.shape[0] // 2
        for j in range(PANELS):
            there = slice(j * NB, (j + 1) * NB)
            for here in (slice(0, depth), slice(depth, 2 * depth)):
                rest = raw[j][here]
                for i in range(j):
                    rest = rest - dot_nt(solved[here, i * NB : (i + 1) * NB], lower[j, i][...])
                solved[here, there] = dot_nt(rest, inverse[j][...])

    depth = out_ref.shape[0]
    product = dot_nn(solved[pl.ds(pl.multiple_of(step * depth, depth), depth), :], across[...])
    head_row = pl.ds(pl.multiple_of(jnp.minimum(my_row, PANELS - 1) * NB, NB), NB)
    head_col = pl.ds(pl.multiple_of(jnp.minimum(my_col, PANELS - 1) * NB, NB), NB)
    for block in range(depth // NB):
        slot = step * (depth // NB) + block
        row = my_row + grid_rows * slot
        here = slice(block * NB, (block + 1) * NB)
        mine = solved[pl.ds(pl.multiple_of(slot * NB, NB), NB), :]
        for t in range(out_ref.shape[1] // NB):
            there = slice(t * NB, (t + 1) * NB)
            updated = matrix_ref[here, there] - product[here, there]
            updated = jnp.where(row < PANELS, 0.0, updated)
            if t == 0:
                panel = mine[:, :NB]
                for j in range(1, PANELS):
                    panel = jnp.where(my_col == j, mine[:, j * NB : (j + 1) * NB], panel)
                factor = jnp.where(my_col <= row, head_ref[head_row, head_col], 0.0)
                panel = jnp.where(row < PANELS, factor, panel)
                updated = jnp.where(my_col < PANELS, panel, updated)
            out_ref[here, there] = updated


def update(grid_rows, place, inverse, head, top, top_other, sent, across, matrix):
    whole = pl.BlockSpec(memory_space=pltpu.VMEM)
    depth = 2 * NB if matrix.shape[0] % (2 * NB) == 0 else NB
    strip = pl.BlockSpec((depth, matrix.shape[1]), lambda step: (step, 0))
    return pl.pallas_call(
        functools.partial(update_kernel, grid_rows),
        out_shape=jax.ShapeDtypeStruct(matrix.shape, jnp.float32),
        grid=(matrix.shape[0] // depth,),
        in_specs=[pl.BlockSpec(memory_space=pltpu.SMEM)] + [whole] * (5 + len(sent)) + [strip],
        out_specs=strip,
        scratch_shapes=[pltpu.VMEM((matrix.shape[0], HEAD), jnp.float32)],
        cost_estimate=pl.CostEstimate(flops=10_000_000_000, bytes_accessed=10_000_000, transcendentals=0),
        compiler_params=pltpu.CompilerParams(vmem_limit_bytes=30 * MIB),
        name="update",
    )(place, inverse, head, top, top_other, *sent, across, matrix)


def body(matrix):
    grid_rows, grid_cols = lax.axis_size("row"), lax.axis_size("col")
    planes = grid_cols // 2
    my_row, my_col = lax.axis_index("row"), lax.axis_index("col")
    plane, core = my_col // 2, my_col % 2

    def send(x, pairs):
        flat = [(a * grid_cols + b, c * grid_cols + d) for (a, b), (c, d) in pairs]
        return lax.ppermute(x, ("row", "col"), flat)

    def swap_cores(x):
        return send(x, [((r, c), (r, c ^ 1)) for r in range(grid_rows) for c in range(grid_cols)])

    def along_rows(x, begin, end):
        out = []
        for d in range(begin, end):
            pairs = [((i, c), (i ^ d, c)) for i in range(PANELS) if i ^ d < grid_rows for c in range(grid_cols)]
            out.append(send(x, pairs) if d else x)
        return out

    place = jnp.stack([my_row, my_col]).astype(jnp.int32)
    corner, matrix = lax.optimization_barrier((matrix[:NB, :NB], matrix))
    carried = jnp.zeros_like(corner)
    passed = []
    for d in [*range(1, planes), 0]:
        pairs = []
        for (i, j), carrier in CARRIED:
            target = 2 * ((j // 2 + d) % planes) + carrier
            if target != j:
                pairs.append(((i, j), (i, target)))
        if d:
            for r in range(PANELS, grid_rows):
                pairs += [((r, q), (r, 2 * d + q)) for q in range(2)]
                pairs.append(((r, 2), (r, 2 * ((1 + d) % planes))))
        passed.append(send(corner, pairs))
        carried = carried + passed[-1]
    native = jnp.zeros((), jnp.bool_)
    for (i, j), carrier in CARRIED:
        if j % 2 == carrier:
            native = native | ((my_row == i) & (my_col == j))
    carried = jnp.where(native, corner, carried)
    heads = along_rows(matrix[:NB], 0, EARLY)
    carried, heads[:2], place = lax.optimization_barrier((carried, heads[:2], place))
    found = along_rows(carried, 0, grid_rows)
    top_mine, top_last = corner, corner
    for d in range(1, planes):
        top_mine = jnp.where(plane == d, passed[d - 1], top_mine)
        top_last = jnp.where((plane - 1) % planes == d, passed[d - 1], top_last)
    found, top, heads = lax.optimization_barrier((found, jnp.stack([top_mine, top_last]), heads))
    mirrored = [swap_cores(x) for x in found]
    strip, _ = lax.optimization_barrier((matrix[NB:, :NB], carried))

    held = strip
    distance = planes // 2
    while distance > 1:
        pairs = []
        for z in range(0, planes, 2 * distance):
            for r in range(grid_rows):
                pairs += [((r, 2 * z + q), (r, 2 * (z + distance) + q)) for q in range(2)]
                pairs.append(((r, 2 * z + 2), (r, 2 * (z + distance) + 2)))
        got = send(held, pairs)
        if distance == 2:
            early, head = factor_head(0, 1, place, *found, *mirrored)
            got, head, late_matrix = lax.optimization_barrier((got, head, matrix))
            heads += along_rows(late_matrix[:NB], EARLY, grid_rows)
        held = jnp.where((plane // distance) % 2 == 1, got, held)
        distance //= 2
    held, head, top = lax.optimization_barrier((held, head, top))
    pairs = []
    for z in range(0, planes, 2):
        for r in range(grid_rows):
            pairs += [((r, 2 * z + q), (r, 2 * z + 2 + q)) for q in range(2)]
            pairs.append(((r, 2 * z + 2), (r, 2 * z)))
    swapped = send(held, pairs)
    held_other, top_other = swap_cores(held), swap_cores(top)
    inverse, head = factor_head(1, HEAD // HALF, place, early, head)
    across = solve_across(0, 1, place, inverse, head, heads)
    swapped, across = lax.optimization_barrier((swapped, across))
    swapped_other = swap_cores(swapped)
    across = solve_across(1, PANELS, place, inverse, head, heads, across)
    sent = [held, held_other, swapped, swapped_other]
    return update(grid_rows, place, inverse, head, top, top_other, sent, across, matrix)


def solution(mesh):
    return jax.shard_map(body, mesh=mesh, in_specs=(P("row", "col"),), out_specs=P("row", "col"), check_vma=False)
```

```python
import functools

import jax
import jax.numpy as jnp
from jax import lax
from jax.experimental import pallas as pl
from jax.experimental.pallas import tpu as pltpu
from jax.sharding import PartitionSpec as P

NB = 256
PANELS = 3
HALF = 128
TILE = 8
STEP = 16
EARLY = 3
HEAD = PANELS * NB
MIB = 1024 * 1024

CARRIED = (((0, 0), 0), ((0, 1), 1), ((1, 2), 0), ((1, 1), 1), ((2, 0), 0), ((2, 2), 1))


def sublane(x, k):
    return jnp.broadcast_to(x[k : k + 1, :], x.shape)


def lane(x, k):
    return jnp.broadcast_to(x[:, k : k + 1], x.shape)


def dot_nt(a, b):
    return lax.dot_general(
        a, b, (((1,), (1,)), ((), ())), precision=lax.Precision.HIGHEST, preferred_element_type=jnp.float32
    )


def dot_nn(a, b):
    return jnp.dot(a, b, precision=lax.Precision.HIGHEST, preferred_element_type=jnp.float32)


def opaque(x):
    return jnp.maximum(x, -3.0e38)


def total(terms):
    while len(terms) > 1:
        terms = [sum(terms[i : i + 2][1:], terms[i]) for i in range(0, len(terms), 2)]
    return terms[0]


def invert_factor(tiles):
    count, wide = len(tiles), STEP // TILE
    rows = lax.broadcasted_iota(jnp.int32, (TILE, HALF), 0)
    lanes = lax.broadcasted_iota(jnp.int32, (TILE, HALF), 1)
    out = []
    for step in range(0, count, wide):
        start, after = TILE * step, step + wide
        own = (lanes >= start) & (lanes < start + STEP)
        column = [[opaque(lane(tiles[step + e], start + k)) for e in range(wide)] for k in range(STEP)]
        forward = [
            jnp.where(own, jnp.where(lanes - start == rows + TILE * e, 1.0, 0.0), tiles[step + e]) for e in range(wide)
        ]
        solved, pivots, below = list(forward), [], {}
        for k in range(0, STEP, 2):
            o, i = k // TILE, k % TILE
            a, b, c = sublane(column[k][o], i), sublane(column[k + 1][o], i), sublane(column[k + 1][o], i + 1)
            det = a * c - b * b
            inverse = pl.reciprocal(det, approx=False)
            pivots.append((a, b, c, det, inverse))
            if k == 0:
                zero = jnp.minimum(jnp.abs(inverse), 0.0)
                for t in range(after, min(after + wide, count)):
                    below[t] = [lane(tiles[t] + zero, start + j) for j in range(STEP)]
            one = [column[k][e] * c - column[k + 1][e] * b for e in range(wide)]
            two = [column[k + 1][e] * a - column[k][e] * b for e in range(wide)]
            pair = (rows == i) | (rows == i + 1)
            one[o], two[o] = jnp.where(pair, 0.0, one[o]), jnp.where(pair, 0.0, two[o])
            first, second = [x * inverse for x in one], [x * inverse for x in two]
            for j in range(k + 2, STEP):
                u, v = sublane(column[j][o], i), sublane(column[j][o], i + 1)
                for e in range(wide):
                    if j < k + 4:
                        column[j][e] = column[j][e] - (one[e] * u + two[e] * v) * inverse
                    else:
                        column[j][e] = column[j][e] - (first[e] * u + second[e] * v)
            u, v = sublane(forward[o], i), sublane(forward[o], i + 1)
            x, y = sublane(solved[o], i), sublane(solved[o], i + 1)
            for e in range(wide):
                if after < count:
                    solved[e] = solved[e] - (first[e] * x + second[e] * y)
                if e > o:
                    forward[e] = forward[e] - (first[e] * u + second[e] * v)
                elif e == o and i + 2 < TILE:
                    forward[e] = forward[e] - jnp.where(rows > i, first[e] * u + second[e] * v, 0.0)
        if after < count:
            right = []
            for k in range(0, STEP, 2):
                o, i = k // TILE, k % TILE
                a, b, c, _, inverse = pivots[k // 2]
                x, y = sublane(solved[o], i), sublane(solved[o], i + 1)
                right += [(x * c - y * b) * inverse, (y * a - x * b) * inverse]
            for t in below:
                tiles[t] = jnp.where(own, 0.0, tiles[t]) - total([below[t][k] * right[k] for k in range(STEP)])
            far = after + wide
            if far < count:
                packed = [jnp.zeros_like(tiles[0])] * count
                for e in range(wide):
                    packed[step + e] = right[TILE * e]
                    for i in range(1, TILE):
                        packed[step + e] = jnp.where(rows == i, right[TILE * e + i], packed[step + e])
                product = dot_nn(jnp.concatenate(tiles[far:], axis=0), jnp.concatenate(packed, axis=0))
                for t in range(far, count):
                    tiles[t] = jnp.where(own, 0.0, tiles[t]) - product[TILE * (t - far) : TILE * (t - far + 1)]
        for e in range(wide):
            diagonal, within = jnp.ones_like(forward[e]), jnp.zeros_like(forward[e])
            for i in range(0, TILE, 2):
                a, b, _, det, _ = pivots[(TILE * e + i) // 2]
                inverse = pl.reciprocal(a, approx=False)
                diagonal = jnp.where(rows == i, a, jnp.where(rows == i + 1, det * inverse, diagonal))
                within = jnp.where(rows == i + 1, b * inverse * sublane(forward[e], i), within)
            out.append((forward[e] - within) * lax.rsqrt(diagonal))
    return out


def assemble(my_row, core, found, mirrored, work):
    for (i, j), carrier in CARRIED:
        for d in range(len(found)):

            @pl.when((my_row ^ i) == d)
            def _():
                block = jnp.where(core == carrier, found[d][...], mirrored[d][...])
                if j > i:
                    work[j * NB : (j + 1) * NB, i * NB : (i + 1) * NB] = block.T
                else:
                    work[i * NB : (i + 1) * NB, j * NB : (j + 1) * NB] = block


def head_kernel(begin, end, place_ref, *refs):
    inverse_ref, work = refs[-2:]
    if begin == 0:
        count = (len(refs) - 2) // 2
        assemble(place_ref[0], place_ref[1] % 2, refs[:count], refs[count : 2 * count], work)
    else:
        inverse_ref[0, :HALF, :HALF] = refs[0][...]
        work[...] = refs[1][...]
    low = lax.broadcasted_iota(jnp.int32, (HALF, HALF), 0) >= lax.broadcasted_iota(jnp.int32, (HALF, HALF), 1)
    for at in range(begin, end):
        left, right = at * HALF, (at + 1) * HALF
        block = work[left:right, left:right]
        tiles = [block[TILE * i : TILE * (i + 1)] for i in range(HALF // TILE)]
        inverse = jnp.where(low, jnp.concatenate(invert_factor(tiles), axis=0), 0.0)
        if begin == 0:
            inverse_ref[...] = inverse
        else:
            diagonal = slice((at % 2) * HALF, (at % 2 + 1) * HALF)
            inverse_ref[at // 2, diagonal, diagonal] = inverse
        work[left:right, left:right] = jnp.where(low, dot_nt(block, inverse), 0.0)
        if right < HEAD:
            solved = dot_nt(work[right:, left:right], inverse)
            work[right:, left:right] = solved
            for column in range(right, HEAD, HALF):
                part = solved[column - right :]
                part = work[column:, column : column + HALF] - dot_nt(part, part[:HALF])
                work[column:, column : column + HALF] = part
        if begin and at % 2:
            k = at // 2
            first, second = inverse_ref[k, :HALF, :HALF], inverse_ref[k, HALF:, HALF:]
            below = work[left:right, left - HALF : left]
            inverse_ref[k, HALF:, :HALF] = -dot_nn(second, dot_nn(below, first))
            inverse_ref[k, :HALF, HALF:] = jnp.zeros((HALF, HALF), jnp.float32)
            work[left - HALF : left, left:right] = jnp.zeros((HALF, HALF), jnp.float32)


def factor_head(begin, end, place, *blocks):
    return pl.pallas_call(
        functools.partial(head_kernel, begin, end),
        out_shape=[
            jax.ShapeDtypeStruct((PANELS, NB, NB) if begin else (HALF, HALF), jnp.float32),
            jax.ShapeDtypeStruct((HEAD, HEAD), jnp.float32),
        ],
        in_specs=[pl.BlockSpec(memory_space=pltpu.SMEM)] + [pl.BlockSpec(memory_space=pltpu.VMEM)] * len(blocks),
        out_specs=[pl.BlockSpec(memory_space=pltpu.VMEM)] * 2,
        cost_estimate=pl.CostEstimate(flops=15_000_000_000 if begin else 1_000, bytes_accessed=1_000, transcendentals=0),
        compiler_params=pltpu.CompilerParams(vmem_limit_bytes=(14 if begin else 48) * MIB),
        name="factor_head",
    )(place, *blocks)


def across_kernel(begin, end, place_ref, inverse_ref, head_ref, *refs):
    heads, across = refs[: len(refs) - 1 - (begin > 0)], refs[-1]
    inverse, lower = head_blocks(inverse_ref, head_ref)
    if begin:
        across[: begin * NB] = refs[-2][...]
    for j in range(begin, end):
        raw = heads[0][...]
        for d in range(1, len(heads)):
            raw = jnp.where((place_ref[0] ^ j) == d, heads[d][...], raw)
        for i in range(j):
            raw = raw - dot_nn(lower[j, i][...], across[i * NB : (i + 1) * NB])
        across[j * NB : (j + 1) * NB] = dot_nn(inverse[j][...], raw)


def head_blocks(inverse_ref, head_ref):
    inverse = [inverse_ref.at[j] for j in range(PANELS)]
    lower = {
        (i, j): head_ref.at[i * NB : (i + 1) * NB, j * NB : (j + 1) * NB] for i, j in ((1, 0), (2, 0), (2, 1))
    }
    return inverse, lower


def solve_across(begin, end, place, inverse, head, heads, *given):
    whole = pl.BlockSpec(memory_space=pltpu.VMEM)
    return pl.pallas_call(
        functools.partial(across_kernel, begin, end),
        out_shape=jax.ShapeDtypeStruct((end * NB, heads[0].shape[1]), jnp.float32),
        in_specs=[pl.BlockSpec(memory_space=pltpu.SMEM)] + [whole] * (2 + len(heads) + len(given)),
        out_specs=whole,
        cost_estimate=pl.CostEstimate(flops=4_000_000_000, bytes_accessed=5_000_000, transcendentals=0),
        compiler_params=pltpu.CompilerParams(vmem_limit_bytes=(20 if len(heads) <= 4 else 56) * MIB),
        name="solve_across",
    )(place, inverse, head, *heads, *given)


def update_kernel(grid_rows, place_ref, inverse_ref, head_ref, top_ref, top_other_ref, *refs):
    held_ref, held_other_ref, swapped_ref, swapped_other_ref, across, matrix_ref, out_ref, solved = refs
    my_row, my_col = place_ref[0], place_ref[1]
    plane, core = my_col // 2, my_col % 2
    step = pl.program_id(0)
    inverse, lower = head_blocks(inverse_ref, head_ref)

    @pl.when(step == 0)
    def _():
        def by_core(mine, other):
            return jnp.where(core == 0, mine, other)

        held, held_other = held_ref[...], held_other_ref[...]
        swapped, swapped_other = swapped_ref[...], swapped_other_ref[...]
        even = plane % 2 == 0
        own, across_core = jnp.where(even, held, swapped), jnp.where(even, held_other, swapped_other)
        last = jnp.where(even, by_core(swapped, swapped_other), by_core(held, held_other))
        first, second, third = top_ref[0], top_other_ref[0], by_core(top_ref[1], top_other_ref[1])
        raw = [
            jnp.concatenate([by_core(first, second), by_core(own, across_core)], axis=0),
            jnp.concatenate([by_core(second, first), by_core(across_core, own)], axis=0),
            jnp.concatenate([third, last], axis=0),
        ]
        depth = solved.shape[0] // 2
        for j in range(PANELS):
            there = slice(j * NB, (j + 1) * NB)
            for here in (slice(0, depth), slice(depth, 2 * depth)):
                rest = raw[j][here]
                for i in range(j):
                    rest = rest - dot_nt(solved[here, i * NB : (i + 1) * NB], lower[j, i][...])
                solved[here, there] = dot_nt(rest, inverse[j][...])

    depth = out_ref.shape[0]
    product = dot_nn(solved[pl.ds(pl.multiple_of(step * depth, depth), depth), :], across[...])
    head_row = pl.ds(pl.multiple_of(jnp.minimum(my_row, PANELS - 1) * NB, NB), NB)
    head_col = pl.ds(pl.multiple_of(jnp.minimum(my_col, PANELS - 1) * NB, NB), NB)
    for block in range(depth // NB):
        slot = step * (depth // NB) + block
        row = my_row + grid_rows * slot
        here = slice(block * NB, (block + 1) * NB)
        mine = solved[pl.ds(pl.multiple_of(slot * NB, NB), NB), :]
        for t in range(out_ref.shape[1] // NB):
            there = slice(t * NB, (t + 1) * NB)
            updated = matrix_ref[here, there] - product[here, there]
            updated = jnp.where(row < PANELS, 0.0, updated)
            if t == 0:
                panel = mine[:, :NB]
                for j in range(1, PANELS):
                    panel = jnp.where(my_col == j, mine[:, j * NB : (j + 1) * NB], panel)
                factor = jnp.where(my_col <= row, head_ref[head_row, head_col], 0.0)
                panel = jnp.where(row < PANELS, factor, panel)
                updated = jnp.where(my_col < PANELS, panel, updated)
            out_ref[here, there] = updated


def update(grid_rows, place, inverse, head, top, top_other, sent, across, matrix):
    whole = pl.BlockSpec(memory_space=pltpu.VMEM)
    depth = 2 * NB if matrix.shape[0] % (2 * NB) == 0 else NB
    if matrix.shape[1] <= 2 * NB:
        depth = matrix.shape[0]
    strip = pl.BlockSpec((depth, matrix.shape[1]), lambda step: (step, 0))
    return pl.pallas_call(
        functools.partial(update_kernel, grid_rows),
        out_shape=jax.ShapeDtypeStruct(matrix.shape, jnp.float32),
        grid=(matrix.shape[0] // depth,),
        in_specs=[pl.BlockSpec(memory_space=pltpu.SMEM)] + [whole] * (5 + len(sent)) + [strip],
        out_specs=strip,
        scratch_shapes=[pltpu.VMEM((matrix.shape[0], HEAD), jnp.float32)],
        cost_estimate=pl.CostEstimate(flops=10_000_000_000, bytes_accessed=10_000_000, transcendentals=0),
        compiler_params=pltpu.CompilerParams(vmem_limit_bytes=30 * MIB),
        name="update",
    )(place, inverse, head, top, top_other, *sent, across, matrix)


def body(matrix):
    grid_rows, grid_cols = lax.axis_size("row"), lax.axis_size("col")
    planes = grid_cols // 2
    my_row, my_col = lax.axis_index("row"), lax.axis_index("col")
    plane, core = my_col // 2, my_col % 2

    def send(x, pairs):
        flat = [(a * grid_cols + b, c * grid_cols + d) for (a, b), (c, d) in pairs]
        return lax.ppermute(x, ("row", "col"), flat)

    def swap_cores(x):
        return send(x, [((r, c), (r, c ^ 1)) for r in range(grid_rows) for c in range(grid_cols)])

    def along_rows(x, begin, end):
        out = []
        for d in range(begin, end):
            pairs = [((i, c), (i ^ d, c)) for i in range(PANELS) if i ^ d < grid_rows for c in range(grid_cols)]
            out.append(send(x, pairs) if d else x)
        return out

    place = jnp.stack([my_row, my_col]).astype(jnp.int32)
    corner, matrix = lax.optimization_barrier((matrix[:NB, :NB], matrix))
    carried = jnp.zeros_like(corner)
    passed = []
    for d in [*range(1, planes), 0]:
        pairs = []
        for (i, j), carrier in CARRIED:
            target = 2 * ((j // 2 + d) % planes) + carrier
            if target != j:
                pairs.append(((i, j), (i, target)))
        if d:
            for r in range(PANELS, grid_rows):
                pairs += [((r, q), (r, 2 * d + q)) for q in range(2)]
                pairs.append(((r, 2), (r, 2 * ((1 + d) % planes))))
        passed.append(send(corner, pairs))
        carried = carried + passed[-1]
    native = jnp.zeros((), jnp.bool_)
    for (i, j), carrier in CARRIED:
        if j % 2 == carrier:
            native = native | ((my_row == i) & (my_col == j))
    carried = jnp.where(native, corner, carried)
    heads = along_rows(matrix[:NB], 0, EARLY)
    carried, heads[:2], place = lax.optimization_barrier((carried, heads[:2], place))
    found = along_rows(carried, 0, grid_rows)
    top_mine, top_last = corner, corner
    for d in range(1, planes):
        top_mine = jnp.where(plane == d, passed[d - 1], top_mine)
        top_last = jnp.where((plane - 1) % planes == d, passed[d - 1], top_last)
    found, top, heads = lax.optimization_barrier((found, jnp.stack([top_mine, top_last]), heads))
    mirrored = [swap_cores(x) for x in found]
    strip, _ = lax.optimization_barrier((matrix[NB:, :NB], carried))

    held = strip
    distance = planes // 2
    while distance > 1:
        pairs = []
        for z in range(0, planes, 2 * distance):
            for r in range(grid_rows):
                pairs += [((r, 2 * z + q), (r, 2 * (z + distance) + q)) for q in range(2)]
                pairs.append(((r, 2 * z + 2), (r, 2 * (z + distance) + 2)))
        got = send(held, pairs)
        if distance == 2:
            early, head = factor_head(0, 1, place, *found, *mirrored)
            got, head, late_matrix = lax.optimization_barrier((got, head, matrix))
            heads += along_rows(late_matrix[:NB], EARLY, grid_rows)
        held = jnp.where((plane // distance) % 2 == 1, got, held)
        distance //= 2
    held, head, top = lax.optimization_barrier((held, head, top))
    pairs = []
    for z in range(0, planes, 2):
        for r in range(grid_rows):
            pairs += [((r, 2 * z + q), (r, 2 * z + 2 + q)) for q in range(2)]
            pairs.append(((r, 2 * z + 2), (r, 2 * z)))
    swapped = send(held, pairs)
    held_other, top_other = swap_cores(held), swap_cores(top)
    inverse, head = factor_head(1, HEAD // HALF, place, early, head)
    across = solve_across(0, 1, place, inverse, head, heads)
    swapped, across = lax.optimization_barrier((swapped, across))
    swapped_other = swap_cores(swapped)
    across = solve_across(1, PANELS, place, inverse, head, heads, across)
    sent = [held, held_other, swapped, swapped_other]
    return update(grid_rows, place, inverse, head, top, top_other, sent, across, matrix)


def solution(mesh):
    return jax.shard_map(body, mesh=mesh, in_specs=(P("row", "col"),), out_specs=P("row", "col"), check_vma=False)
```
